32 devices in a mesh: pool: 16 (over z, y, x), tensor: 2 (over core).
Axes of the slice: x: 2, y: 2, z: 4, core: 2. Of those that a mesh axis runs over, the one named last changes fastest.
Arguments:
- tokens: bfloat16 [2, 256, 8192], P(None, None, 'tensor'), may hold values from -6 to 6
- gate_up_weight: bfloat16 [8192, 2, 28672], P('tensor', None, 'pool'), may hold values from -0.0625 to 0.0625
- down_weight: bfloat16 [28672, 8192], P('pool', 'tensor'), may hold values from -0.03125 to 0.03125
- shrink_store: bfloat16 [16, 2, 8192, 64], P('pool', None, 'tensor'), may hold values from -0.0625 to 0.0625
- expand_store: bfloat16 [16, 2, 64, 28672], P('pool', None, 'tensor'), may hold values from -0.75 to 0.75
- block_adapter: int32 [2, 2], replicated, may hold values from 0 to 15
- block_live: int32 [2, 2], replicated, may hold values from 1 to 128, 192 in all within a row
- adapter_slot: int32 [16], replicated, may hold values from 0 to 15, each once
Outputs:
- layer_out: bfloat16 [2, 256, 8192], P(None, 'pool', 'tensor')
The draws below stay inside these ranges and needn't reach their ends.
Inputs may be any that keep to these rules, and one draw needn't show every extreme that they name: Each storage slot holds exactly one adapter; adapter a is stored on index adapter_slot[a] of pool; each index of pool holds exactly one storage slot. `block_live`: rows of a block after its live rows are padding; the live rows of one decode step sum to 192.
All inputs are finite; a program needn't handle non-finite values.
Results may differ from the reference program's by a relative error of at most 0.0049.
Values may be sent and summed in bfloat16 or wider, within the bound.
No kernel may reach another device: no remote copies, remote signals or barrier semaphores. Data moves between devices by JAX's collectives and lax.ppermute only.
A program may use at most 192 MiB of HBM per device.

```python
import math
import jax
import jax.numpy as jnp
import numpy as np
from jax import lax

D = 8192
FF = 28672
RANK = 64
BLK = 128
STEPS = 2
NBLK = 2
ROWS = 256
NADP = 16


def touch_ends(array, rng, smallest, top_value):
    place = [jax.random.randint(jax.random.fold_in(rng, axis), (), 0, length) for axis, length in enumerate(array.shape)]
    longest = array.shape.index(max(array.shape))
    neighbour = place[:longest] + [(place[longest] + 1) % array.shape[longest]] + place[longest + 1:]
    return array.at[tuple(place)].set(smallest).at[tuple(neighbour)].set(top_value)


def block_levels(key, dims, split, low, top_value):
    def one(dim, parts):
        steps = jax.random.uniform(jax.random.fold_in(jax.random.fold_in(key, 6), dim), (parts,), jnp.float32, low / len(split), top_value / len(split))
        return jnp.repeat(jnp.exp(steps), dims[dim] // parts).reshape((-1,) + (1,) * (len(dims) - dim - 1))

    factor_of = one(*split[0])
    for cut in split[1:]:
        factor_of = factor_of * one(*cut)
    return factor_of


def rank_table(amount, skew):
    weights = [(1 << 20) // math.isqrt(standing ** skew) + 1 for standing in range(1, amount + 1)]
    scale = 1 + sum(weights) // (1 << 30)
    return np.cumsum(np.array([max(1, weight // scale) for weight in weights]))


def skewed_ids(rng, extent, amount, lean):
    grid = rank_table(amount, lean)
    pick = jax.random.randint(jax.random.fold_in(rng, 1), extent, 0, int(grid[amount - 1]))
    standing = jnp.searchsorted(jnp.asarray(grid, jnp.int32), pick, side="right")
    return jax.random.permutation(jax.random.fold_in(rng, 2), amount)[standing].astype(jnp.int32)


def profile(number_of, total, bound, lean):
    loads = [(1 << 20) // math.isqrt(grade ** lean) + 1 for grade in range(2, number_of + 1)]
    rest, holding = total - bound - (number_of - 1), [1] * (number_of - 1)
    while rest > 0:
        movable = [i for i in range(number_of - 1) if holding[i] < bound]
        whole, remaining = sum([loads[i] for i in movable]), rest
        for i in movable:
            more = min(bound - holding[i], max(1, remaining * loads[i] // whole), rest)
            holding[i] = holding[i] + more
            rest = rest - more
    return np.array([bound] + holding)


def ragged(stream_key, number_of, total, bound, slope):
    if number_of == 2:
        one = jax.random.randint(stream_key, (), max(1, total - bound), min(bound, total - 1) + 1)
        return jnp.stack([one, total - one])
    lengths = jnp.asarray(profile(number_of, total, bound, slope), jnp.int32)
    twos = (number_of - 1) // 2
    donor, taker = lengths[1:1 + 2 * twos:2], lengths[2:2 + 2 * twos:2]
    slack = jnp.minimum(donor - 1, bound - taker)
    passed = jax.random.randint(jax.random.fold_in(stream_key, 1), (twos,), 0, 1 << 20) % (slack + 1)
    lengths = lengths.at[1:1 + 2 * twos:2].set(donor - passed).at[2:2 + 2 * twos:2].set(taker + passed)
    return lengths[jax.random.permutation(jax.random.fold_in(stream_key, 2), number_of)]


def scatter_about(rng, shape, scale, bound, cuts=(), held_as=jnp.bfloat16):
    array = jax.random.normal(rng, shape, jnp.float32) * scale
    if len(cuts) > 0:
        array = block_levels(rng, shape, cuts, -0.22, 0.18) * array
    return jnp.clip(array, min=-bound, max=bound).astype(held_as)


def setup_inputs(seed: int = 0) -> dict:
    keys = jax.random.split(jax.random.key(seed), 9)
    return {
        "tokens": scatter_about(keys[0], (STEPS, ROWS, D), 1.0, 6.0, ((2, 2),)),
        "gate_up_weight": scatter_about(keys[1], (D, 2, FF), D ** -0.5, 0.0625, ((0, 2), (2, 16))),
        "down_weight": scatter_about(keys[2], (FF, D), FF ** -0.5, 0.03125, ((0, 16), (1, 2))),
        "shrink_store": scatter_about(keys[3], (NADP, 2, D, RANK), D ** -0.5, 0.0625, ((0, 16), (2, 2))),
        "expand_store": scatter_about(keys[4], (NADP, 2, RANK, FF), RANK ** -0.5, 0.75, ((0, 16), (2, 2))),
        "block_adapter": touch_ends(skewed_ids(keys[5], (STEPS, NBLK), NADP, 2), jax.random.fold_in(keys[5], 3), 0, NADP - 1).astype(jnp.int32),
        "block_live": jax.vmap(lambda own: ragged(own, NBLK, BLK + (NBLK - 1) * BLK // 2, BLK, 0))(jax.random.split(keys[6], STEPS)).reshape((STEPS, NBLK)).astype(jnp.int32),
        "adapter_slot": jax.random.permutation(keys[7], NADP).astype(jnp.int32),
    }


def reference(tokens, gate_up_weight, down_weight, shrink_store, expand_store, block_adapter, block_live, adapter_slot):
    highest = lax.Precision.HIGHEST
    flat_weight = gate_up_weight.reshape(D, 2 * FF)
    row_index = jnp.arange(ROWS)
    outputs = []
    for decode_step in range(STEPS):
        inputs = tokens[decode_step]
        pieces = []
        for block_index in range(NBLK):
            slot = adapter_slot[block_adapter[decode_step, block_index]]
            first = shrink_store[slot].astype(jnp.float32)
            second = expand_store[slot].astype(jnp.float32)
            block_rows = inputs[block_index * BLK:(block_index + 1) * BLK].astype(jnp.float32)
            shrunk = jnp.einsum("nd,kdc->knc", block_rows, first, precision=highest)
            pieces.append(jnp.einsum("knc,kcf->nkf", shrunk, second, precision=highest))
        adapted = jnp.concatenate(pieces, axis=0)
        gate_up = jnp.dot(inputs, flat_weight, preferred_element_type=jnp.float32).reshape(ROWS, 2, FF) + adapted
        hidden = (jax.nn.silu(gate_up[:, 0]) * gate_up[:, 1]).astype(jnp.bfloat16)
        owners = row_index // BLK
        live = jnp.sum((owners[:, None] == jnp.arange(NBLK)[None, :]) * block_live[decode_step][None, :], axis=1)
        keep = ((row_index % BLK) < live).astype(jnp.float32)
        summed = jnp.dot(hidden, down_weight, preferred_element_type=jnp.float32)
        outputs.append((summed * keep[:, None]).astype(jnp.bfloat16))
    return jnp.stack(outputs)
```

```python
import jax
import jax.numpy as jnp
from jax import lax
from jax.sharding import PartitionSpec as P

BLK = 128
NBLK = 2


def pool_reduce(part, order):
    count = lax.axis_size("pool")
    me = lax.axis_index("pool")
    bits = count.bit_length() - 1
    rows, cols = part.shape
    current = part.reshape((2,) * bits + (rows // count, cols))
    left = list(reversed(range(bits)))
    for bit in order:
        axis = left.index(bit)
        left.remove(bit)
        mine = (me >> bit) & 1
        keep = lax.dynamic_index_in_dim(current, mine, axis, keepdims=False)
        send = lax.dynamic_index_in_dim(current, 1 - mine, axis, keepdims=False)
        got = lax.ppermute(
            send.astype(jnp.bfloat16), "pool", [(i, i ^ (1 << bit)) for i in range(count)]
        )
        current = keep + got.astype(jnp.float32)
    return current


def shards(
    tokens,
    gate_up_weight,
    down_weight,
    shrink_store,
    expand_store,
    block_adapter,
    block_live,
    adapter_slot,
):
    steps, total_rows, width_local = tokens.shape
    units = gate_up_weight.shape[2]
    pool_count = lax.axis_size("pool")
    tensor_count = lax.axis_size("tensor")
    me = lax.axis_index("pool")
    kinds = gate_up_weight.shape[1]
    ranks_local = expand_store.shape[2]
    rank = ranks_local * tensor_count
    units_here = units // tensor_count
    rows_here = total_rows // pool_count
    bits = pool_count.bit_length() - 1
    slots = adapter_slot[block_adapter]

    outgoing = expand_store[0].reshape(kinds, ranks_local, pool_count * tensor_count, units_here)
    outgoing = outgoing.transpose(2, 0, 1, 3)
    second = lax.all_to_all(outgoing, ("pool", "tensor"), split_axis=0, concat_axis=0, tiled=True)
    second = second.reshape(pool_count, tensor_count, kinds, ranks_local, units_here)

    first = jnp.einsum(
        "snd,kdc->snkc", tokens, shrink_store[0], preferred_element_type=jnp.float32
    )
    mine = jnp.repeat((slots == me).astype(jnp.float32), total_rows // NBLK, axis=1)
    shrunk = lax.psum(first * mine[:, :, None, None], ("pool", "tensor"))

    flat_tokens = tokens.reshape(steps * total_rows, width_local)
    grouped = gate_up_weight.reshape(width_local // 8, 8, kinds, units).transpose(0, 2, 1, 3)
    partial_sums = jnp.stack(
        [
            jnp.dot(
                flat_tokens,
                grouped[:, kind].reshape(width_local, units),
                preferred_element_type=jnp.float32,
            )
            for kind in range(kinds)
        ]
    )
    main = lax.psum_scatter(partial_sums, "tensor", scatter_dimension=2, tiled=True)
    main = main.reshape(kinds, steps, NBLK, BLK, units_here)
    shrunk = shrunk.reshape(steps, NBLK, BLK, kinds, rank)
    high = shrunk.astype(jnp.bfloat16)
    low = (shrunk - high.astype(jnp.float32)).astype(jnp.bfloat16)
    shrunk = jnp.concatenate([high, low], axis=4)
    hidden_blocks = []
    for step in range(steps):
        for block in range(NBLK):
            page = lax.dynamic_index_in_dim(second, slots[step, block], 0, keepdims=False)
            page = page.transpose(1, 0, 2, 3).reshape(kinds, rank, units_here)
            gate, up = [
                main[kind, step, block]
                + jnp.dot(
                    shrunk[step, block, :, kind],
                    jnp.concatenate([page[kind], page[kind]], axis=0),
                    preferred_element_type=jnp.float32,
                )
                for kind in range(kinds)
            ]
            hidden_blocks.append((jax.nn.silu(gate) * up).astype(jnp.bfloat16))
    hidden = lax.all_gather(jnp.concatenate(hidden_blocks, axis=0), "tensor", axis=1, tiled=True)

    positions = me * rows_here + jnp.arange(rows_here)
    owners = positions // BLK
    half = down_weight.shape[1] // 2
    orders = [list(range(bits)), [1, 0] + list(range(2, bits))]
    results = []
    for step in range(steps):
        live = jnp.sum(
            (owners[:, None] == jnp.arange(NBLK)[None, :]) * block_live[step][None, :], axis=1
        )
        keep = (positions % BLK < live).astype(jnp.float32)
        pieces = []
        for piece in range(2):
            part = jnp.dot(
                hidden[step * total_rows : (step + 1) * total_rows],
                down_weight[:, piece * half : (piece + 1) * half],
                preferred_element_type=jnp.float32,
            )
            pieces.append(pool_reduce(part, orders[piece]))
        summed = jnp.concatenate(pieces, axis=1)
        results.append((summed * keep[:, None]).astype(jnp.bfloat16))
    return jnp.stack(results)


def solution(mesh):
    return jax.shard_map(
        shards,
        mesh=mesh,
        in_specs=(
            P(None, None, "tensor"),
            P("tensor", None, "pool"),
            P("pool", "tensor"),
            P("pool", None, "tensor", None),
            P("pool", None, "tensor", None),
            P(),
            P(),
            P(),
        ),
        out_specs=P(None, "pool", "tensor"),
        check_vma=False,
    )
```

```python
import jax
import jax.numpy as jnp
from jax import lax
from jax.sharding import PartitionSpec as P

BLK = 128
NBLK = 2


def bit_pairs(axis_name, bit):
    return [(i, i ^ (1 << bit)) for i in range(lax.axis_size(axis_name))]


def halve(array, axis_name, bit, axis, wire=None):
    mine = (lax.axis_index(axis_name) >> bit) & 1
    keep = lax.dynamic_index_in_dim(array, mine, axis, keepdims=False)
    send = lax.dynamic_index_in_dim(array, 1 - mine, axis, keepdims=False)
    if wire is not None:
        send = send.astype(wire)
    return keep, send


def swap(array, axis_name, bit):
    return lax.ppermute(array, axis_name, bit_pairs(axis_name, bit))


def bits_of(axis_name):
    return lax.axis_size(axis_name).bit_length() - 1


def scatter_sum(array, axis_name, axis):
    count = bits_of(axis_name)
    shape = array.shape
    length = shape[axis] >> count
    current = array.reshape(shape[:axis] + (2,) * count + (length,) + shape[axis + 1 :])
    for bit in reversed(range(count)):
        keep, send = halve(current, axis_name, bit, axis)
        current = keep + swap(send, axis_name, bit)
    return current


def gather(array, axis_name, axis):
    for bit in range(bits_of(axis_name)):
        mine = (lax.axis_index(axis_name) >> bit) & 1
        got = swap(array, axis_name, bit)
        array = jnp.where(
            mine == 0,
            jnp.concatenate([array, got], axis=axis),
            jnp.concatenate([got, array], axis=axis),
        )
    return array


def sum_all(array, axis_name):
    for bit in range(bits_of(axis_name)):
        array = array + swap(array, axis_name, bit)
    return array


PLANE_BITS = 2
ROUND = 2


def after(array, arrived):
    return lax.optimization_barrier((array, arrived))[0]


def plane_pages(store, arrived, history):
    kinds, ranks, count, cols = store.shape
    width = min(PLANE_BITS, bits_of("pool"))
    held = []
    orders = []
    for kind in range(kinds):
        orders.append([(kind + turn) % width for turn in range(width)])
        held.append({0: store[kind].reshape((ranks, count >> width) + (2,) * width + (cols,))})
    left = [list(reversed(range(width))) for _ in range(kinds)]
    for turn in range(width):
        sends = []
        for kind in range(kinds):
            bit = orders[kind][turn]
            axis = 2 + left[kind].index(bit)
            left[kind].remove(bit)
            split = {place: halve(page, "pool", bit, axis) for place, page in held[kind].items()}
            held[kind] = {place: keep for place, (keep, _) in split.items()}
            sends.append(jnp.stack([send for _, send in split.values()]))
        if arrived is not None and turn == 0:
            sends = after(sends, arrived)
        arrived = []
        for kind in range(kinds):
            bit = orders[kind][turn]
            got = swap(sends[kind], "pool", bit)
            arrived.append(got)
            for row, place in enumerate(list(held[kind])):
                held[kind][place | (1 << bit)] = got[row]
        history.append(arrived)
    pages = [
        [held[kind][place] for kind in range(kinds)] for place in range(1 << width)
    ]
    return pages, arrived


def plane_exchange(pages, chosen):
    me = lax.axis_index("pool")
    width = min(PLANE_BITS, bits_of("pool"))
    planes = lax.axis_size("pool") >> width
    plane = me >> width
    out = []
    for apart in range(planes):
        target = plane ^ apart
        columns = [
            [lax.dynamic_index_in_dim(page, target, 1, keepdims=False) for page in kinds_of]
            for kinds_of in pages
        ]
        picked = jnp.stack(
            [
                jnp.stack(
                    [
                        lax.select_n(choice, *[one[kind] for one in columns])
                        for kind in range(len(pages[0]))
                    ]
                )
                for choice in chosen
            ]
        )
        if apart:
            pairs = [(i, i ^ (apart << width)) for i in range(lax.axis_size("pool"))]
            picked = lax.ppermute(picked, "pool", pairs)
        out.append(picked)
    return out


def shards(
    tokens,
    gate_up_weight,
    down_weight,
    shrink_store,
    expand_store,
    block_adapter,
    block_live,
    adapter_slot,
):
    steps, total_rows, width_local = tokens.shape
    units = gate_up_weight.shape[2]
    pool_count = lax.axis_size("pool")
    tensor_count = lax.axis_size("tensor")
    me = lax.axis_index("pool")
    core = lax.axis_index("tensor")
    kinds = gate_up_weight.shape[1]
    ranks_local = expand_store.shape[2]
    rank = ranks_local * tensor_count
    units_here = units // tensor_count
    rows_here = total_rows // pool_count
    slots = adapter_slot[block_adapter]

    width = min(PLANE_BITS, bits_of("pool"))
    plane_size = 1 << width
    needed = jnp.any(
        slots.reshape(-1)[:, None] == jnp.arange(pool_count)[None, :], axis=0
    ).reshape(-1, plane_size)
    order = jnp.cumsum(needed.astype(jnp.int32), axis=1) - 1
    mine_needed = lax.dynamic_index_in_dim(needed, me >> width, 0, keepdims=False)
    mine_order = lax.dynamic_index_in_dim(order, me >> width, 0, keepdims=False)
    place = me & (plane_size - 1)

    def choice(number):
        hit = mine_needed & (mine_order == number)
        return jnp.sum(jnp.where(hit, jnp.arange(plane_size) ^ place, 0)).astype(jnp.int32)

    store = expand_store[0].reshape(kinds, ranks_local, pool_count, units)
    half_ranks = ranks_local // 2
    arrived = None
    page_sets = []
    history = []
    for part in range(2):
        pages, arrived = plane_pages(
            store[:, part * half_ranks : (part + 1) * half_ranks], arrived, history
        )
        page_sets.append(pages)
    block_number = order.reshape(-1)[slots]
    block_apart = (slots >> width) ^ (me >> width)

    def exchange(first_number):
        chosen = [choice(first_number + m) for m in range(ROUND)]
        sets = [plane_exchange(pages, chosen) for pages in page_sets]
        arrays = [
            jnp.concatenate([one[apart] for one in sets], axis=2) for apart in range(len(sets[0]))
        ]
        everything = jnp.concatenate(arrays, axis=0)
        found = [
            lax.dynamic_index_in_dim(
                everything,
                block_apart[step, block] * ROUND
                + jnp.clip(block_number[step, block] - first_number, 0, ROUND - 1),
                0,
                keepdims=False,
            )
            for step in range(steps)
            for block in range(NBLK)
        ]
        return jnp.stack(found)

    found = exchange(0)
    first = jnp.einsum(
        "snd,kdc->snkc", tokens, shrink_store[0], preferred_element_type=jnp.float32
    )
    mine = jnp.repeat((slots == me).astype(jnp.float32), total_rows // NBLK, axis=1)
    first = first * mine[:, :, None, None]
    first = first.reshape(steps * total_rows, kinds * rank)
    shrunk = gather(sum_all(scatter_sum(first, "tensor", 0), "pool"), "tensor", 0)
    high = shrunk.astype(jnp.bfloat16)
    low = (shrunk - high.astype(jnp.float32)).astype(jnp.bfloat16)

    flat_tokens = tokens.reshape(steps * total_rows, width_local)

    weights = after(gate_up_weight, history[width - 1])
    weights = lax.optimization_barrier(jnp.transpose(weights, (1, 0, 2)))
    main = []
    for kind in range(kinds):
        flat_tokens = after(flat_tokens, history[min(width + kind, len(history) - 1)])
        product = lax.optimization_barrier(
            jnp.dot(flat_tokens, weights[kind], preferred_element_type=jnp.float32)
        )
        if tensor_count == 2:
            low_share, high_share = product[:, :units_here], product[:, units_here:]
            sent = swap(jnp.where(core == 0, high_share, low_share), "tensor", 0)
            main.append(jnp.where(core == 0, low_share, high_share) + sent)
        else:
            main.append(scatter_sum(product, "tensor", 1))

    found, main, high, low = lax.optimization_barrier((found, main, high, low))
    if plane_size > ROUND:
        later = (block_number >= ROUND).reshape(-1)

        def more(found):
            return jnp.where(later[:, None, None, None], exchange(ROUND), found)

        found = lax.cond(jnp.any(later), more, lambda found: found, found)
    found = found.reshape(steps, NBLK, kinds, ranks_local, tensor_count, units_here)

    bits = bits_of("pool")
    positions = me * rows_here + jnp.arange(rows_here)
    owners = positions // BLK
    half = down_weight.shape[1] // 2
    orders = [list(range(bits)), [1, 0] + list(range(2, bits))]
    sums = []
    arrived = None
    for step in range(steps):
        second = found[step]
        tensor_bits = bits_of("tensor")
        second = second.reshape(
            (NBLK, kinds, ranks_local) + (2,) * tensor_bits + (units_here,)
        )
        for bit in range(tensor_bits):
            keep, send = halve(second, "tensor", bit, second.ndim - 2)
            got = swap(send, "tensor", bit)
            second = jnp.where(
                ((core >> bit) & 1) == 0,
                jnp.concatenate([keep, got], axis=2),
                jnp.concatenate([got, keep], axis=2),
            )
        hidden_blocks = []
        for block in range(NBLK):
            page = second[block]
            rows = slice(step * total_rows + block * BLK, step * total_rows + (block + 1) * BLK)
            gate, up = [
                main[kind][rows]
                + jnp.dot(
                    jnp.concatenate(
                        [part[rows, kind * rank : (kind + 1) * rank] for part in (high, low)], axis=1
                    ),
                    jnp.concatenate([page[kind], page[kind]], axis=0),
                    preferred_element_type=jnp.float32,
                )
                for kind in range(kinds)
            ]
            hidden_blocks.append((jax.nn.silu(gate) * up).astype(jnp.bfloat16))
        hidden = gather(jnp.concatenate(hidden_blocks, axis=0), "tensor", 1)
        parts = [
            jnp.dot(
                hidden,
                down_weight[:, piece * half : (piece + 1) * half],
                preferred_element_type=jnp.float32,
            ).reshape((2,) * bits + (rows_here, half))
            for piece in range(2)
        ]
        pairs = [
            halve(parts[piece], "pool", orders[piece][0], bits - 1 - orders[piece][0], jnp.bfloat16)
            for piece in range(2)
        ]
        sends = [send for _, send in pairs]
        if arrived is not None:
            sends, _ = lax.optimization_barrier((sends, arrived))
        arrived = [swap(sends[piece], "pool", orders[piece][0]) for piece in range(2)]
        sums.append([pairs[piece][0] + arrived[piece].astype(jnp.float32) for piece in range(2)])
    results = []
    for step in range(steps):
        pieces = []
        for piece in range(2):
            current = sums[step][piece]
            remaining = list(reversed(range(bits)))
            remaining.remove(orders[piece][0])
            for bit in orders[piece][1:]:
                keep, send = halve(current, "pool", bit, remaining.index(bit), jnp.bfloat16)
                remaining.remove(bit)
                current = keep + swap(send, "pool", bit).astype(jnp.float32)
            pieces.append(current)
        live = jnp.sum(
            (owners[:, None] == jnp.arange(NBLK)[None, :]) * block_live[step][None, :], axis=1
        )
        keep = (positions % BLK < live).astype(jnp.float32)
        summed = jnp.concatenate(pieces, axis=1)
        results.append((summed * keep[:, None]).astype(jnp.bfloat16))
    return jnp.stack(results)


def solution(mesh):
    return jax.shard_map(
        shards,
        mesh=mesh,
        in_specs=(
            P(None, None, "tensor"),
            P("tensor", None, "pool"),
            P("pool", "tensor"),
            P("pool", None, "tensor", None),
            P("pool", None, "tensor", None),
            P(),
            P(),
            P(),
        ),
        out_specs=P(None, "pool", "tensor"),
        check_vma=False,
    )
```

```python
import jax
import jax.numpy as jnp
from jax import lax
from jax.sharding import PartitionSpec as P

BLK = 128
NBLK = 2


def bit_pairs(axis_name, bit):
    return [(i, i ^ (1 << bit)) for i in range(lax.axis_size(axis_name))]


def halve(array, axis_name, bit, axis, wire=None):
    mine = (lax.axis_index(axis_name) >> bit) & 1
    keep = lax.dynamic_index_in_dim(array, mine, axis, keepdims=False)
    send = lax.dynamic_index_in_dim(array, 1 - mine, axis, keepdims=False)
    if wire is not None:
        send = send.astype(wire)
    return keep, send


def swap(array, axis_name, bit):
    return lax.ppermute(array, axis_name, bit_pairs(axis_name, bit))


def bits_of(axis_name):
    return lax.axis_size(axis_name).bit_length() - 1


def scatter_sum(array, axis_name, axis):
    count = bits_of(axis_name)
    shape = array.shape
    length = shape[axis] >> count
    current = array.reshape(shape[:axis] + (2,) * count + (length,) + shape[axis + 1 :])
    for bit in reversed(range(count)):
        keep, send = halve(current, axis_name, bit, axis)
        current = keep + swap(send, axis_name, bit)
    return current


def gather(array, axis_name, axis):
    for bit in range(bits_of(axis_name)):
        mine = (lax.axis_index(axis_name) >> bit) & 1
        got = swap(array, axis_name, bit)
        array = jnp.where(
            mine == 0,
            jnp.concatenate([array, got], axis=axis),
            jnp.concatenate([got, array], axis=axis),
        )
    return array


PLANE_BITS = 2
ROUND = 2


def after(array, arrived):
    return lax.optimization_barrier((array, arrived))[0]


def plane_pages(store, arrived, sent):
    kinds, ranks, count, cols = store.shape
    width = min(PLANE_BITS, bits_of("pool"))
    held = []
    orders = []
    for kind in range(kinds):
        orders.append([(kind + turn) % width for turn in range(width)])
        held.append({0: store[kind].reshape((ranks, count >> width) + (2,) * width + (cols,))})
    left = [list(reversed(range(width))) for _ in range(kinds)]
    for turn in range(width):
        sends = []
        for kind in range(kinds):
            bit = orders[kind][turn]
            axis = 2 + left[kind].index(bit)
            left[kind].remove(bit)
            split = {place: halve(page, "pool", bit, axis) for place, page in held[kind].items()}
            held[kind] = {place: keep for place, (keep, _) in split.items()}
            sends.append(jnp.stack([send for _, send in split.values()]))
        if arrived is not None and turn == 0:
            sends = after(sends, arrived)
        sent.append(sends)
        arrived = []
        for kind in range(kinds):
            bit = orders[kind][turn]
            got = swap(sends[kind], "pool", bit)
            arrived.append(got)
            for row, place in enumerate(list(held[kind])):
                held[kind][place | (1 << bit)] = got[row]
    pages = [
        [held[kind][place] for kind in range(kinds)] for place in range(1 << width)
    ]
    return pages, arrived


def plane_exchange(pages, chosen, gate=None):
    width = min(PLANE_BITS, bits_of("pool"))
    count = lax.axis_size("pool")
    planes = count >> width
    plane = lax.axis_index("pool") >> width
    out = [None] * planes
    early, late = [], []
    for apart in reversed(range(planes)):
        columns = [
            [lax.dynamic_index_in_dim(page, plane ^ apart, 1, keepdims=False) for page in kinds_of]
            for kinds_of in pages
        ]
        picked = jnp.stack(
            [
                jnp.stack(
                    [
                        lax.select_n(choice, *[one[kind] for one in columns])
                        for kind in range(len(pages[0]))
                    ]
                )
                for choice in chosen
            ]
        )
        if apart == 1 and gate is not None:
            picked = after(picked, gate)
        if apart:
            (late if apart == 1 else early).append(picked)
            pairs = [(i, i ^ (apart << width)) for i in range(count)]
            picked = lax.ppermute(picked, "pool", pairs)
        out[apart] = picked
    return out, early, late


def shards(
    tokens,
    gate_up_weight,
    down_weight,
    shrink_store,
    expand_store,
    block_adapter,
    block_live,
    adapter_slot,
):
    steps, total_rows, width_local = tokens.shape
    units = gate_up_weight.shape[2]
    pool_count = lax.axis_size("pool")
    tensor_count = lax.axis_size("tensor")
    me = lax.axis_index("pool")
    core = lax.axis_index("tensor")
    kinds = gate_up_weight.shape[1]
    ranks_local = expand_store.shape[2]
    rank = ranks_local * tensor_count
    units_here = units // tensor_count
    rows_here = total_rows // pool_count
    slots = adapter_slot[block_adapter]

    width = min(PLANE_BITS, bits_of("pool"))
    plane_size = 1 << width
    needed = jnp.any(
        slots.reshape(-1)[:, None] == jnp.arange(pool_count)[None, :], axis=0
    ).reshape(-1, plane_size)
    order = jnp.cumsum(needed.astype(jnp.int32), axis=1) - 1
    mine_needed = lax.dynamic_index_in_dim(needed, me >> width, 0, keepdims=False)
    mine_order = lax.dynamic_index_in_dim(order, me >> width, 0, keepdims=False)
    place = me & (plane_size - 1)

    def choice(number):
        hit = mine_needed & (mine_order == number)
        return jnp.sum(jnp.where(hit, jnp.arange(plane_size) ^ place, 0)).astype(jnp.int32)

    store = expand_store[0].reshape(kinds, ranks_local, pool_count, units)
    half_ranks = ranks_local // 2
    arrived = None
    page_sets = []
    sent = []
    for part in range(2):
        pages, arrived = plane_pages(
            store[:, part * half_ranks : (part + 1) * half_ranks], arrived, sent
        )
        page_sets.append(pages)
    block_number = order.reshape(-1)[slots]
    block_apart = (slots >> width) ^ (me >> width)

    def exchange(first_number, gates):
        chosen = [choice(first_number + m) for m in range(ROUND)]
        sets, early, late = zip(
            *[plane_exchange(pages, chosen, gate) for pages, gate in zip(page_sets, gates)]
        )
        arrays = [
            jnp.concatenate([one[apart] for one in sets], axis=2) for apart in range(len(sets[0]))
        ]
        everything = jnp.concatenate(arrays, axis=0)
        found = [
            lax.dynamic_index_in_dim(
                everything,
                block_apart[step, block] * ROUND
                + jnp.clip(block_number[step, block] - first_number, 0, ROUND - 1),
                0,
                keepdims=False,
            )
            for step in range(steps)
            for block in range(NBLK)
        ]
        return jnp.stack(found), sets, early, late

    found, page_parts, early, late = exchange(0, (sent[2 * width - 1], None))
    first = jnp.einsum(
        "snd,kdc->snkc", after(tokens, sent[0]), shrink_store[0], preferred_element_type=jnp.float32
    )
    mine = jnp.repeat((slots == me).astype(jnp.float32), total_rows // NBLK, axis=1)
    first = first * mine[:, :, None, None]
    first = first.reshape(steps * total_rows, kinds * rank)
    shrunk = after(scatter_sum(first, "tensor", 0), sent[width - 1])

    def sum_over(shrunk, some_bits):
        for bit in some_bits:
            shrunk = shrunk + swap(shrunk, "pool", bit)
        return shrunk

    shrunk = sum_over(shrunk, range(width))
    flat_tokens = tokens.reshape(steps * total_rows, width_local)

    weights = after(gate_up_weight, (early[0], sent[width]))
    weights = jnp.transpose(weights, (1, 0, 2))
    shrunk, weights, _ = lax.optimization_barrier((shrunk, weights, sent[2 * width - 1]))
    last = bits_of("pool") - 1
    shrunk = sum_over(shrunk, range(width, last))
    gates = [(sent[2 * width - 1], late[0]), (early[1], late[1], page_parts[0])]
    products = []
    for kind in range(kinds):
        flat_tokens = after(flat_tokens, gates[kind])
        product = jnp.dot(flat_tokens, weights[kind], preferred_element_type=jnp.float32)
        product, shrunk, flat_tokens = lax.optimization_barrier((product, shrunk, flat_tokens))
        products.append(product)
        if kind == 0:
            shrunk = after(shrunk, (early[1], late[1]))
            shrunk = sum_over(shrunk, range(last, last + 1))
    products = after(products, page_parts[1])
    main = []
    for product in products:
        if tensor_count == 2:
            low_share, high_share = product[:, :units_here], product[:, units_here:]
            got = swap(jnp.where(core == 0, high_share, low_share), "tensor", 0)
            main.append(jnp.where(core == 0, low_share, high_share) + got)
        else:
            main.append(scatter_sum(product, "tensor", 1))

    shrunk = gather(shrunk, "tensor", 0)
    high = shrunk.astype(jnp.bfloat16)
    low = (shrunk - high.astype(jnp.float32)).astype(jnp.bfloat16)

    found, main, high, low = lax.optimization_barrier((found, main, high, low))
    if plane_size > ROUND:
        later = (block_number >= ROUND).reshape(-1)

        def more(found):
            return jnp.where(later[:, None, None, None], exchange(ROUND, (None, None))[0], found)

        found = lax.cond(jnp.any(later), more, lambda found: found, found)
    found = found.reshape(steps, NBLK, kinds, ranks_local, tensor_count, units_here)

    bits = bits_of("pool")
    positions = me * rows_here + jnp.arange(rows_here)
    owners = positions // BLK
    half = down_weight.shape[1] // 2
    orders = [list(range(bits)), [1, 0] + list(range(2, bits))]
    parts = []
    for step in range(steps):
        second = found[step]
        tensor_bits = bits_of("tensor")
        second = second.reshape(
            (NBLK, kinds, ranks_local) + (2,) * tensor_bits + (units_here,)
        )
        for bit in range(tensor_bits):
            keep, send = halve(second, "tensor", bit, second.ndim - 2)
            got = swap(send, "tensor", bit)
            second = jnp.where(
                ((core >> bit) & 1) == 0,
                jnp.concatenate([keep, got], axis=2),
                jnp.concatenate([got, keep], axis=2),
            )
        hidden_blocks = []
        for block in range(NBLK):
            page = second[block]
            rows = slice(step * total_rows + block * BLK, step * total_rows + (block + 1) * BLK)
            gate, up = [
                main[kind][rows]
                + jnp.dot(
                    jnp.concatenate(
                        [part[rows, kind * rank : (kind + 1) * rank] for part in (high, low)], axis=1
                    ),
                    jnp.concatenate([page[kind], page[kind]], axis=0),
                    preferred_element_type=jnp.float32,
                )
                for kind in range(kinds)
            ]
            hidden_blocks.append((jax.nn.silu(gate) * up).astype(jnp.bfloat16))
        hidden = gather(jnp.concatenate(hidden_blocks, axis=0), "tensor", 1)
        parts.append(
            [
                jnp.dot(
                    hidden,
                    down_weight[:, piece * half : (piece + 1) * half],
                    preferred_element_type=jnp.float32,
                ).reshape((2,) * bits + (rows_here, half))
                for piece in range(2)
            ]
        )

    kept = [[None] * 2 for _ in range(steps)]
    sends = [[None] * 2 for _ in range(steps)]
    arrived = [None] * steps

    def prepare(step, stage):
        for piece in range(2):
            left = sorted(orders[piece][stage:], reverse=True)
            bit = orders[piece][stage]
            kept[step][piece], sends[step][piece] = halve(
                parts[step][piece], "pool", bit, left.index(bit), jnp.bfloat16
            )

    def exchange_rows(step, stage):
        arrived[step] = [
            swap(sends[step][piece], "pool", orders[piece][stage]) for piece in range(2)
        ]
        parts[step] = [
            kept[step][piece] + arrived[step][piece].astype(jnp.float32) for piece in range(2)
        ]

    for stage in range(bits):
        for step in range(steps):
            prepare(step, stage)
            if stage == 0 and step:
                sends[step] = after(sends[step], arrived[step - 1])
            if stage == bits - 1 and step == 0:
                sends[step] = after(sends[step], later_sends)
            if stage == 1 and step == steps - 1:
                later_sends = list(sends[step])
            exchange_rows(step, stage)
    results = []
    for step in range(steps):
        live = jnp.sum(
            (owners[:, None] == jnp.arange(NBLK)[None, :]) * block_live[step][None, :], axis=1
        )
        keep = (positions % BLK < live).astype(jnp.float32)
        summed = jnp.concatenate(parts[step], axis=1)
        results.append((summed * keep[:, None]).astype(jnp.bfloat16))
    return jnp.stack(results)


def solution(mesh):
    return jax.shard_map(
        shards,
        mesh=mesh,
        in_specs=(
            P(None, None, "tensor"),
            P("tensor", None, "pool"),
            P("pool", "tensor"),
            P("pool", None, "tensor", None),
            P("pool", None, "tensor", None),
            P(),
            P(),
            P(),
        ),
        out_specs=P(None, "pool", "tensor"),
        check_vma=False,
    )
```

```python
import jax
import jax.numpy as jnp
from jax import lax
from jax.sharding import PartitionSpec as P

BLK = 128
NBLK = 2


def bit_pairs(axis_name, bit):
    return [(i, i ^ (1 << bit)) for i in range(lax.axis_size(axis_name))]


def halve(array, axis_name, bit, axis, wire=None):
    mine = (lax.axis_index(axis_name) >> bit) & 1
    keep = lax.dynamic_index_in_dim(array, mine, axis, keepdims=False)
    send = lax.dynamic_index_in_dim(array, 1 - mine, axis, keepdims=False)
    if wire is not None:
        send = send.astype(wire)
    return keep, send


def swap(array, axis_name, bit):
    return lax.ppermute(array, axis_name, bit_pairs(axis_name, bit))


def bits_of(axis_name):
    return lax.axis_size(axis_name).bit_length() - 1


def scatter_sum(array, axis_name, axis):
    count = bits_of(axis_name)
    shape = array.shape
    length = shape[axis] >> count
    current = array.reshape(shape[:axis] + (2,) * count + (length,) + shape[axis + 1 :])
    for bit in reversed(range(count)):
        keep, send = halve(current, axis_name, bit, axis)
        current = keep + swap(send, axis_name, bit)
    return current


def gather(array, axis_name, axis):
    for bit in range(bits_of(axis_name)):
        mine = (lax.axis_index(axis_name) >> bit) & 1
        got = swap(array, axis_name, bit)
        array = jnp.where(
            mine == 0,
            jnp.concatenate([array, got], axis=axis),
            jnp.concatenate([got, array], axis=axis),
        )
    return array


def after(array, arrived):
    return lax.optimization_barrier((array, arrived))[0]


def shards(
    tokens,
    gate_up_weight,
    down_weight,
    shrink_store,
    expand_store,
    block_adapter,
    block_live,
    adapter_slot,
):
    steps, total_rows, width_local = tokens.shape
    units = gate_up_weight.shape[2]
    pool_count = lax.axis_size("pool")
    tensor_count = lax.axis_size("tensor")
    me = lax.axis_index("pool")
    core = lax.axis_index("tensor")
    kinds = gate_up_weight.shape[1]
    ranks_local = expand_store.shape[2]
    rank = ranks_local * tensor_count
    units_here = units // tensor_count
    rows_here = total_rows // pool_count
    slots = adapter_slot[block_adapter]

    second = []
    outgoing = []
    for kind in range(kinds):
        columns = expand_store[0, kind].reshape(ranks_local, pool_count * tensor_count, units_here)
        columns = columns.transpose(1, 0, 2)
        if second:
            columns = after(columns, second[-1])
        outgoing.append(columns)
        second.append(
            lax.all_to_all(columns, ("pool", "tensor"), split_axis=0, concat_axis=0, tiled=True)
        )
    pages = [one.reshape(pool_count, rank, units_here) for one in second]

    first = jnp.einsum(
        "snd,kdc->snkc",
        after(tokens, outgoing[0]),
        shrink_store[0],
        preferred_element_type=jnp.float32,
    )
    mine = jnp.repeat((slots == me).astype(jnp.float32), total_rows // NBLK, axis=1)
    first = first * mine[:, :, None, None]
    first = first.reshape(steps * total_rows, kinds * rank)
    shrunk = scatter_sum(first, "tensor", 0)

    def sum_over(shrunk, some_bits):
        for bit in some_bits:
            shrunk = shrunk + swap(shrunk, "pool", bit)
        return shrunk

    middle = bits_of("pool") // 2
    shrunk = sum_over(shrunk, range(middle))

    flat_tokens = tokens.reshape(steps * total_rows, width_local)

    weights = after(gate_up_weight, outgoing[0])
    weights = jnp.transpose(weights, (1, 0, 2))
    weights, shrunk, flat_tokens, _ = lax.optimization_barrier(
        (weights, shrunk, flat_tokens, second[0])
    )
    shrunk = sum_over(shrunk, range(middle, bits_of("pool")))
    products = [
        jnp.dot(flat_tokens, weights[kind], preferred_element_type=jnp.float32)
        for kind in range(kinds)
    ]
    products[-1] = after(products[-1], second[-1])
    main = []
    for product in products:
        if tensor_count == 2:
            low_share, high_share = product[:, :units_here], product[:, units_here:]
            got = swap(jnp.where(core == 0, high_share, low_share), "tensor", 0)
            main.append(jnp.where(core == 0, low_share, high_share) + got)
        else:
            main.append(scatter_sum(product, "tensor", 1))

    shrunk = gather(shrunk, "tensor", 0)
    high = shrunk.astype(jnp.bfloat16)
    low = (shrunk - high.astype(jnp.float32)).astype(jnp.bfloat16)

    bits = bits_of("pool")
    positions = me * rows_here + jnp.arange(rows_here)
    owners = positions // BLK
    half = down_weight.shape[1] // 2
    orders = [list(range(bits)), [1, 0] + list(range(2, bits))]
    parts = []
    for step in range(steps):
        hidden_blocks = []
        for block in range(NBLK):
            page = [
                lax.dynamic_index_in_dim(one, slots[step, block], 0, keepdims=False)
                for one in pages
            ]
            rows = slice(step * total_rows + block * BLK, step * total_rows + (block + 1) * BLK)
            gate, up = [
                main[kind][rows]
                + jnp.dot(
                    jnp.concatenate(
                        [part[rows, kind * rank : (kind + 1) * rank] for part in (high, low)], axis=1
                    ),
                    jnp.concatenate([page[kind], page[kind]], axis=0),
                    preferred_element_type=jnp.float32,
                )
                for kind in range(kinds)
            ]
            hidden_blocks.append((jax.nn.silu(gate) * up).astype(jnp.bfloat16))
        hidden = gather(jnp.concatenate(hidden_blocks, axis=0), "tensor", 1)
        parts.append(
            [
                jnp.dot(
                    hidden,
                    down_weight[:, piece * half : (piece + 1) * half],
                    preferred_element_type=jnp.float32,
                ).reshape((2,) * bits + (rows_here, half))
                for piece in range(2)
            ]
        )

    kept = [[None] * 2 for _ in range(steps)]
    sends = [[None] * 2 for _ in range(steps)]
    arrived = [None] * steps

    def prepare(step, stage):
        for piece in range(2):
            left = sorted(orders[piece][stage:], reverse=True)
            bit = orders[piece][stage]
            kept[step][piece], sends[step][piece] = halve(
                parts[step][piece], "pool", bit, left.index(bit), jnp.bfloat16
            )

    def exchange_rows(step, stage):
        arrived[step] = [
            swap(sends[step][piece], "pool", orders[piece][stage]) for piece in range(2)
        ]
        parts[step] = [
            kept[step][piece] + arrived[step][piece].astype(jnp.float32) for piece in range(2)
        ]

    for stage in range(bits):
        for step in range(steps):
            prepare(step, stage)
            if stage == 0 and step:
                sends[step] = after(sends[step], arrived[step - 1])
            if stage == bits - 1 and step == 0:
                sends[step] = after(sends[step], later_sends)
            if stage == 1 and step == steps - 1:
                later_sends = list(sends[step])
            exchange_rows(step, stage)
    results = []
    for step in range(steps):
        live = jnp.sum(
            (owners[:, None] == jnp.arange(NBLK)[None, :]) * block_live[step][None, :], axis=1
        )
        keep = (positions % BLK < live).astype(jnp.float32)
        summed = jnp.concatenate(parts[step], axis=1)
        results.append((summed * keep[:, None]).astype(jnp.bfloat16))
    return jnp.stack(results)


def solution(mesh):
    return jax.shard_map(
        shards,
        mesh=mesh,
        in_specs=(
            P(None, None, "tensor"),
            P("tensor", None, "pool"),
            P("pool", "tensor"),
            P("pool", None, "tensor", None),
            P("pool", None, "tensor", None),
            P(),
            P(),
            P(),
        ),
        out_specs=P(None, "pool", "tensor"),
        check_vma=False,
    )
```

```python
import jax
import jax.numpy as jnp
from jax import lax
from jax.sharding import PartitionSpec as P

BLK = 128
NBLK = 2


def bit_pairs(axis_name, bit):
    return [(i, i ^ (1 << bit)) for i in range(lax.axis_size(axis_name))]


def halve(array, axis_name, bit, axis, wire=None):
    mine = (lax.axis_index(axis_name) >> bit) & 1
    keep = lax.dynamic_index_in_dim(array, mine, axis, keepdims=False)
    send = lax.dynamic_index_in_dim(array, 1 - mine, axis, keepdims=False)
    if wire is not None:
        send = send.astype(wire)
    return keep, send


def swap(array, axis_name, bit):
    return lax.ppermute(array, axis_name, bit_pairs(axis_name, bit))


def bits_of(axis_name):
    return lax.axis_size(axis_name).bit_length() - 1


def scatter_sum(array, axis_name, axis):
    count = bits_of(axis_name)
    shape = array.shape
    length = shape[axis] >> count
    current = array.reshape(shape[:axis] + (2,) * count + (length,) + shape[axis + 1 :])
    for bit in reversed(range(count)):
        keep, send = halve(current, axis_name, bit, axis)
        current = keep + swap(send, axis_name, bit)
    return current


def gather(array, axis_name, axis):
    for bit in range(bits_of(axis_name)):
        mine = (lax.axis_index(axis_name) >> bit) & 1
        got = swap(array, axis_name, bit)
        array = jnp.where(
            mine == 0,
            jnp.concatenate([array, got], axis=axis),
            jnp.concatenate([got, array], axis=axis),
        )
    return array


def after(array, arrived):
    return lax.optimization_barrier((array, arrived))[0]


def shards(
    tokens,
    gate_up_weight,
    down_weight,
    shrink_store,
    expand_store,
    block_adapter,
    block_live,
    adapter_slot,
):
    steps, total_rows, width_local = tokens.shape
    units = gate_up_weight.shape[2]
    pool_count = lax.axis_size("pool")
    tensor_count = lax.axis_size("tensor")
    me = lax.axis_index("pool")
    core = lax.axis_index("tensor")
    kinds = gate_up_weight.shape[1]
    ranks_local = expand_store.shape[2]
    rank = ranks_local * tensor_count
    units_here = units // tensor_count
    rows_here = total_rows // pool_count
    slots = adapter_slot[block_adapter]

    outgoing = expand_store[0].reshape(kinds, ranks_local, pool_count * tensor_count, units_here)
    outgoing = outgoing.transpose(2, 0, 1, 3)
    second = lax.all_to_all(outgoing, ("pool", "tensor"), split_axis=0, concat_axis=0, tiled=True)
    second = second.reshape(pool_count, tensor_count, kinds, ranks_local, units_here)

    first = jnp.einsum(
        "snd,kdc->snkc",
        after(tokens, outgoing),
        shrink_store[0],
        preferred_element_type=jnp.float32,
    )
    mine = jnp.repeat((slots == me).astype(jnp.float32), total_rows // NBLK, axis=1)
    first = first * mine[:, :, None, None]
    first = first.reshape(steps * total_rows, kinds * rank)
    shrunk = scatter_sum(first, "tensor", 0)

    def sum_over(shrunk, some_bits):
        for bit in some_bits:
            shrunk = shrunk + swap(shrunk, "pool", bit)
        return shrunk

    middle = bits_of("pool") // 2
    shrunk = sum_over(shrunk, range(middle))

    flat_tokens = tokens.reshape(steps * total_rows, width_local)

    weights = after(gate_up_weight, outgoing)
    weights = jnp.transpose(weights, (1, 0, 2))
    weights, shrunk, flat_tokens = lax.optimization_barrier((weights, shrunk, flat_tokens))
    shrunk = sum_over(shrunk, range(middle, bits_of("pool")))
    products = [
        jnp.dot(flat_tokens, weights[kind], preferred_element_type=jnp.float32)
        for kind in range(kinds)
    ]
    products = lax.optimization_barrier(products)
    main = []
    for product in products:
        if tensor_count == 2:
            low_share, high_share = product[:, :units_here], product[:, units_here:]
            got = swap(jnp.where(core == 0, high_share, low_share), "tensor", 0)
            main.append(jnp.where(core == 0, low_share, high_share) + got)
        else:
            main.append(scatter_sum(product, "tensor", 1))

    shrunk = gather(shrunk, "tensor", 0)
    high = shrunk.astype(jnp.bfloat16)
    low = (shrunk - high.astype(jnp.float32)).astype(jnp.bfloat16)

    bits = bits_of("pool")
    positions = me * rows_here + jnp.arange(rows_here)
    owners = positions // BLK
    half = down_weight.shape[1] // 2
    orders = [list(range(bits)), [1, 0] + list(range(2, bits))]
    parts = []
    for step in range(steps):
        hidden_blocks = []
        for block in range(NBLK):
            page = lax.dynamic_index_in_dim(second, slots[step, block], 0, keepdims=False)
            page = page.transpose(1, 0, 2, 3).reshape(kinds, rank, units_here)
            rows = slice(step * total_rows + block * BLK, step * total_rows + (block + 1) * BLK)
            gate, up = [
                main[kind][rows]
                + jnp.dot(
                    jnp.concatenate(
                        [part[rows, kind * rank : (kind + 1) * rank] for part in (high, low)], axis=1
                    ),
                    jnp.concatenate([page[kind], page[kind]], axis=0),
                    preferred_element_type=jnp.float32,
                )
                for kind in range(kinds)
            ]
            hidden_blocks.append((jax.nn.silu(gate) * up).astype(jnp.bfloat16))
        hidden = gather(jnp.concatenate(hidden_blocks, axis=0), "tensor", 1)
        parts.append(
            [
                jnp.dot(
                    hidden,
                    down_weight[:, piece * half : (piece + 1) * half],
                    preferred_element_type=jnp.float32,
                ).reshape((2,) * bits + (rows_here, half))
                for piece in range(2)
            ]
        )

    kept = [[None] * 2 for _ in range(steps)]
    sends = [[None] * 2 for _ in range(steps)]
    arrived = [None] * steps

    def prepare(step, stage):
        for piece in range(2):
            left = sorted(orders[piece][stage:], reverse=True)
            bit = orders[piece][stage]
            kept[step][piece], sends[step][piece] = halve(
                parts[step][piece], "pool", bit, left.index(bit), jnp.bfloat16
            )

    def exchange_rows(step, stage):
        arrived[step] = [
            swap(sends[step][piece], "pool", orders[piece][stage]) for piece in range(2)
        ]
        parts[step] = [
            kept[step][piece] + arrived[step][piece].astype(jnp.float32) for piece in range(2)
        ]

    for stage in range(bits):
        for step in range(steps):
            prepare(step, stage)
            if stage == 0 and step:
                sends[step] = after(sends[step], arrived[step - 1])
            if stage == bits - 1 and step == 0:
                sends[step] = after(sends[step], later_sends)
            if stage == 1 and step == steps - 1:
                later_sends = list(sends[step])
            exchange_rows(step, stage)
    results = []
    for step in range(steps):
        live = jnp.sum(
            (owners[:, None] == jnp.arange(NBLK)[None, :]) * block_live[step][None, :], axis=1
        )
        keep = (positions % BLK < live).astype(jnp.float32)
        summed = jnp.concatenate(parts[step], axis=1)
        results.append((summed * keep[:, None]).astype(jnp.bfloat16))
    return jnp.stack(results)


def solution(mesh):
    return jax.shard_map(
        shards,
        mesh=mesh,
        in_specs=(
            P(None, None, "tensor"),
            P("tensor", None, "pool"),
            P("pool", "tensor"),
            P("pool", None, "tensor", None),
            P("pool", None, "tensor", None),
            P(),
            P(),
            P(),
        ),
        out_specs=P(None, "pool", "tensor"),
        check_vma=False,
    )
```

```python
import jax
import jax.numpy as jnp
from jax import lax
from jax.sharding import PartitionSpec as P

BLK = 128
NBLK = 2


def bit_pairs(axis_name, bit):
    return [(i, i ^ (1 << bit)) for i in range(lax.axis_size(axis_name))]


def halve(array, axis_name, bit, axis, wire=None):
    mine = (lax.axis_index(axis_name) >> bit) & 1
    keep = lax.dynamic_index_in_dim(array, mine, axis, keepdims=False)
    send = lax.dynamic_index_in_dim(array, 1 - mine, axis, keepdims=False)
    if wire is not None:
        send = send.astype(wire)
    return keep, send


def swap(array, axis_name, bit):
    return lax.ppermute(array, axis_name, bit_pairs(axis_name, bit))


def bits_of(axis_name):
    return lax.axis_size(axis_name).bit_length() - 1


def scatter_sum(array, axis_name, axis):
    count = bits_of(axis_name)
    shape = array.shape
    length = shape[axis] >> count
    current = array.reshape(shape[:axis] + (2,) * count + (length,) + shape[axis + 1 :])
    for bit in reversed(range(count)):
        keep, send = halve(current, axis_name, bit, axis)
        current = keep + swap(send, axis_name, bit)
    return current


def gather(array, axis_name, axis):
    for bit in range(bits_of(axis_name)):
        mine = (lax.axis_index(axis_name) >> bit) & 1
        got = swap(array, axis_name, bit)
        array = jnp.where(
            mine == 0,
            jnp.concatenate([array, got], axis=axis),
            jnp.concatenate([got, array], axis=axis),
        )
    return array


def after(array, arrived):
    return lax.optimization_barrier((array, arrived))[0]


def shards(
    tokens,
    gate_up_weight,
    down_weight,
    shrink_store,
    expand_store,
    block_adapter,
    block_live,
    adapter_slot,
):
    steps, total_rows, width_local = tokens.shape
    units = gate_up_weight.shape[2]
    pool_count = lax.axis_size("pool")
    tensor_count = lax.axis_size("tensor")
    me = lax.axis_index("pool")
    core = lax.axis_index("tensor")
    kinds = gate_up_weight.shape[1]
    ranks_local = expand_store.shape[2]
    rank = ranks_local * tensor_count
    units_here = units // tensor_count
    rows_here = total_rows // pool_count
    slots = adapter_slot[block_adapter]

    second = []
    outgoing = []
    for kind in range(kinds):
        columns = expand_store[0, kind].reshape(ranks_local, pool_count * tensor_count, units_here)
        columns = columns.transpose(1, 0, 2)
        if second:
            columns = after(columns, second[-1])
        outgoing.append(columns)
        second.append(
            lax.all_to_all(columns, ("pool", "tensor"), split_axis=0, concat_axis=0, tiled=True)
        )
    pages = [one.reshape(pool_count, rank, units_here) for one in second]

    first = jnp.einsum(
        "snd,kdc->snkc",
        after(tokens, outgoing[0]),
        shrink_store[0],
        preferred_element_type=jnp.float32,
    )
    mine = jnp.repeat((slots == me).astype(jnp.float32), total_rows // NBLK, axis=1)
    first = first * mine[:, :, None, None]
    first = first.reshape(steps * total_rows, kinds * rank)
    shrunk = scatter_sum(first, "tensor", 0)

    def sum_over(shrunk, some_bits):
        for bit in some_bits:
            shrunk = shrunk + swap(shrunk, "pool", bit)
        return shrunk

    middle = bits_of("pool") // 2
    shrunk = sum_over(shrunk, range(middle))

    flat_tokens = tokens.reshape(steps * total_rows, width_local)

    weights = after(gate_up_weight, outgoing[0])
    weights = jnp.transpose(weights, (1, 0, 2))
    weights, shrunk, flat_tokens, _ = lax.optimization_barrier(
        (weights, shrunk, flat_tokens, second[0])
    )
    shrunk = sum_over(shrunk, range(middle, bits_of("pool")))
    products = [
        jnp.dot(flat_tokens, weights[kind], preferred_element_type=jnp.float32)
        for kind in range(kinds)
    ]
    products = lax.optimization_barrier(products)
    main = []
    for product in products:
        if tensor_count == 2:
            low_share, high_share = product[:, :units_here], product[:, units_here:]
            got = swap(jnp.where(core == 0, high_share, low_share), "tensor", 0)
            main.append(jnp.where(core == 0, low_share, high_share) + got)
        else:
            main.append(scatter_sum(product, "tensor", 1))

    shrunk = gather(shrunk, "tensor", 0)
    high = shrunk.astype(jnp.bfloat16)
    low = (shrunk - high.astype(jnp.float32)).astype(jnp.bfloat16)

    bits = bits_of("pool")
    positions = me * rows_here + jnp.arange(rows_here)
    owners = positions // BLK
    half = down_weight.shape[1] // 2
    orders = [list(range(bits)), [1, 0] + list(range(2, bits))]
    parts = []
    for step in range(steps):
        hidden_blocks = []
        for block in range(NBLK):
            page = [
                lax.dynamic_index_in_dim(one, slots[step, block], 0, keepdims=False)
                for one in pages
            ]
            rows = slice(step * total_rows + block * BLK, step * total_rows + (block + 1) * BLK)
            gate, up = [
                main[kind][rows]
                + jnp.dot(
                    jnp.concatenate(
                        [part[rows, kind * rank : (kind + 1) * rank] for part in (high, low)], axis=1
                    ),
                    jnp.concatenate([page[kind], page[kind]], axis=0),
                    preferred_element_type=jnp.float32,
                )
                for kind in range(kinds)
            ]
            hidden_blocks.append((jax.nn.silu(gate) * up).astype(jnp.bfloat16))
        hidden = gather(jnp.concatenate(hidden_blocks, axis=0), "tensor", 1)
        parts.append(
            [
                jnp.dot(
                    hidden,
                    down_weight[:, piece * half : (piece + 1) * half],
                    preferred_element_type=jnp.float32,
                ).reshape((2,) * bits + (rows_here, half))
                for piece in range(2)
            ]
        )

    kept = [[None] * 2 for _ in range(steps)]
    sends = [[None] * 2 for _ in range(steps)]
    arrived = [None] * steps

    def prepare(step, stage):
        for piece in range(2):
            left = sorted(orders[piece][stage:], reverse=True)
            bit = orders[piece][stage]
            kept[step][piece], sends[step][piece] = halve(
                parts[step][piece], "pool", bit, left.index(bit), jnp.bfloat16
            )

    def exchange_rows(step, stage):
        arrived[step] = [
            swap(sends[step][piece], "pool", orders[piece][stage]) for piece in range(2)
        ]
        parts[step] = [
            kept[step][piece] + arrived[step][piece].astype(jnp.float32) for piece in range(2)
        ]

    for stage in range(bits):
        for step in range(steps):
            prepare(step, stage)
            if stage == 0 and step:
                sends[step] = after(sends[step], arrived[step - 1])
            if stage == 2 and step == 0:
                sends[step] = after(sends[step], later_sends)
            if stage == 1 and step == steps - 1:
                later_sends = list(sends[step])
            exchange_rows(step, stage)
    results = []
    for step in range(steps):
        live = jnp.sum(
            (owners[:, None] == jnp.arange(NBLK)[None, :]) * block_live[step][None, :], axis=1
        )
        keep = (positions % BLK < live).astype(jnp.float32)
        summed = jnp.concatenate(parts[step], axis=1)
        results.append((summed * keep[:, None]).astype(jnp.bfloat16))
    return jnp.stack(results)


def solution(mesh):
    return jax.shard_map(
        shards,
        mesh=mesh,
        in_specs=(
            P(None, None, "tensor"),
            P("tensor", None, "pool"),
            P("pool", "tensor"),
            P("pool", None, "tensor", None),
            P("pool", None, "tensor", None),
            P(),
            P(),
            P(),
        ),
        out_specs=P(None, "pool", "tensor"),
        check_vma=False,
    )
```

```python
import jax
import jax.numpy as jnp
from jax import lax
from jax.sharding import PartitionSpec as P

BLK = 128
NBLK = 2


def bit_pairs(axis_name, bit):
    return [(i, i ^ (1 << bit)) for i in range(lax.axis_size(axis_name))]


def halve(array, axis_name, bit, axis, wire=None):
    mine = (lax.axis_index(axis_name) >> bit) & 1
    keep = lax.dynamic_index_in_dim(array, mine, axis, keepdims=False)
    send = lax.dynamic_index_in_dim(array, 1 - mine, axis, keepdims=False)
    if wire is not None:
        send = send.astype(wire)
    return keep, send


def swap(array, axis_name, bit):
    return lax.ppermute(array, axis_name, bit_pairs(axis_name, bit))


def bits_of(axis_name):
    return lax.axis_size(axis_name).bit_length() - 1


def scatter_sum(array, axis_name, axis):
    count = bits_of(axis_name)
    shape = array.shape
    length = shape[axis] >> count
    current = array.reshape(shape[:axis] + (2,) * count + (length,) + shape[axis + 1 :])
    for bit in reversed(range(count)):
        keep, send = halve(current, axis_name, bit, axis)
        current = keep + swap(send, axis_name, bit)
    return current


def gather(array, axis_name, axis):
    for bit in range(bits_of(axis_name)):
        mine = (lax.axis_index(axis_name) >> bit) & 1
        got = swap(array, axis_name, bit)
        array = jnp.where(
            mine == 0,
            jnp.concatenate([array, got], axis=axis),
            jnp.concatenate([got, array], axis=axis),
        )
    return array


def after(array, arrived):
    return lax.optimization_barrier((array, arrived))[0]


def shards(
    tokens,
    gate_up_weight,
    down_weight,
    shrink_store,
    expand_store,
    block_adapter,
    block_live,
    adapter_slot,
):
    steps, total_rows, width_local = tokens.shape
    units = gate_up_weight.shape[2]
    pool_count = lax.axis_size("pool")
    tensor_count = lax.axis_size("tensor")
    me = lax.axis_index("pool")
    core = lax.axis_index("tensor")
    kinds = gate_up_weight.shape[1]
    ranks_local = expand_store.shape[2]
    rank = ranks_local * tensor_count
    units_here = units // tensor_count
    rows_here = total_rows // pool_count
    slots = adapter_slot[block_adapter]

    second = []
    outgoing = []
    for kind in range(kinds):
        columns = expand_store[0, kind].reshape(ranks_local, pool_count * tensor_count, units_here)
        columns = columns.transpose(1, 0, 2)
        if second:
            columns = after(columns, second[-1])
        outgoing.append(columns)
        second.append(
            lax.all_to_all(columns, ("pool", "tensor"), split_axis=0, concat_axis=0, tiled=True)
        )
    pages = [one.reshape(pool_count, rank, units_here) for one in second]

    first = jnp.einsum(
        "snd,kdc->snkc",
        after(tokens, outgoing[0]),
        shrink_store[0],
        preferred_element_type=jnp.float32,
    )
    mine = jnp.repeat((slots == me).astype(jnp.float32), total_rows // NBLK, axis=1)
    first = first * mine[:, :, None, None]
    first = first.reshape(steps * total_rows, kinds * rank)
    shrunk = scatter_sum(first, "tensor", 0)

    def sum_over(shrunk, some_bits):
        for bit in some_bits:
            shrunk = shrunk + swap(shrunk, "pool", bit)
        return shrunk

    middle = bits_of("pool") // 2
    shrunk = sum_over(shrunk, range(middle))

    flat_tokens = tokens.reshape(steps * total_rows, width_local)

    weights = after(gate_up_weight, outgoing[0])
    weights = jnp.transpose(weights, (1, 0, 2))
    weights, shrunk, flat_tokens, _ = lax.optimization_barrier(
        (weights, shrunk, flat_tokens, second[0])
    )
    bits = bits_of("pool")
    products = []
    for kind in range(kinds):
        got = swap(shrunk, "pool", middle + kind)
        products.append(
            jnp.dot(flat_tokens, weights[kind], preferred_element_type=jnp.float32)
        )
        products, got, flat_tokens = lax.optimization_barrier((products, got, flat_tokens))
        shrunk = shrunk + got
    main = []
    for product in products:
        if tensor_count == 2:
            low_share, high_share = product[:, :units_here], product[:, units_here:]
            got = swap(jnp.where(core == 0, high_share, low_share), "tensor", 0)
            main.append(jnp.where(core == 0, low_share, high_share) + got)
        else:
            main.append(scatter_sum(product, "tensor", 1))

    shrunk = sum_over(shrunk, range(middle + kinds, bits))
    shrunk = gather(shrunk, "tensor", 0)
    high = shrunk.astype(jnp.bfloat16)
    low = (shrunk - high.astype(jnp.float32)).astype(jnp.bfloat16)

    positions = me * rows_here + jnp.arange(rows_here)
    owners = positions // BLK
    half = down_weight.shape[1] // 2
    orders = [list(range(bits)), [1, 0] + list(range(2, bits))]
    parts = []
    for step in range(steps):
        hidden_blocks = []
        for block in range(NBLK):
            page = [
                lax.dynamic_index_in_dim(one, slots[step, block], 0, keepdims=False)
                for one in pages
            ]
            rows = slice(step * total_rows + block * BLK, step * total_rows + (block + 1) * BLK)
            gate, up = [
                main[kind][rows]
                + jnp.dot(
                    jnp.concatenate(
                        [part[rows, kind * rank : (kind + 1) * rank] for part in (high, low)], axis=1
                    ),
                    jnp.concatenate([page[kind], page[kind]], axis=0),
                    preferred_element_type=jnp.float32,
                )
                for kind in range(kinds)
            ]
            hidden_blocks.append((jax.nn.silu(gate) * up).astype(jnp.bfloat16))
        hidden = gather(jnp.concatenate(hidden_blocks, axis=0), "tensor", 1)
        parts.append(
            [
                jnp.dot(
                    hidden,
                    down_weight[:, piece * half : (piece + 1) * half],
                    preferred_element_type=jnp.float32,
                ).reshape((2,) * bits + (rows_here, half))
                for piece in range(2)
            ]
        )

    kept = [[None] * 2 for _ in range(steps)]
    sends = [[None] * 2 for _ in range(steps)]
    arrived = [None] * steps

    def prepare(step, stage):
        if stage == 2:
            parts[step] = [jnp.concatenate(parts[step], axis=-1)]
        kept[step] = [None] * len(parts[step])
        sends[step] = [None] * len(parts[step])
        for piece in range(len(parts[step])):
            left = sorted(orders[piece][stage:], reverse=True)
            bit = orders[piece][stage]
            kept[step][piece], sends[step][piece] = halve(
                parts[step][piece], "pool", bit, left.index(bit), jnp.bfloat16
            )

    def exchange_rows(step, stage):
        arrived[step] = [
            swap(sends[step][piece], "pool", orders[piece][stage])
            for piece in range(len(sends[step]))
        ]
        parts[step] = [
            mine + got.astype(jnp.float32) for mine, got in zip(kept[step], arrived[step])
        ]

    for stage in range(bits):
        for step in range(steps):
            prepare(step, stage)
            if stage == 0 and step:
                sends[step] = after(sends[step], arrived[step - 1])
            if stage == 2 and step == 0:
                sends[step] = after(sends[step], later_sends)
            if stage == 1 and step == steps - 1:
                later_sends = list(sends[step])
            exchange_rows(step, stage)
    results = []
    for step in range(steps):
        live = jnp.sum(
            (owners[:, None] == jnp.arange(NBLK)[None, :]) * block_live[step][None, :], axis=1
        )
        keep = (positions % BLK < live).astype(jnp.float32)
        summed = parts[step][0]
        results.append((summed * keep[:, None]).astype(jnp.bfloat16))
    return jnp.stack(results)


def solution(mesh):
    return jax.shard_map(
        shards,
        mesh=mesh,
        in_specs=(
            P(None, None, "tensor"),
            P("tensor", None, "pool"),
            P("pool", "tensor"),
            P("pool", None, "tensor", None),
            P("pool", None, "tensor", None),
            P(),
            P(),
            P(),
        ),
        out_specs=P(None, "pool", "tensor"),
        check_vma=False,
    )
```

```python
import jax
import jax.numpy as jnp
from jax import lax
from jax.sharding import PartitionSpec as P

BLK = 128
NBLK = 2


def bit_pairs(axis_name, bit):
    return [(i, i ^ (1 << bit)) for i in range(lax.axis_size(axis_name))]


def halve(array, axis_name, bit, axis, wire=None):
    mine = (lax.axis_index(axis_name) >> bit) & 1
    keep = lax.dynamic_index_in_dim(array, mine, axis, keepdims=False)
    send = lax.dynamic_index_in_dim(array, 1 - mine, axis, keepdims=False)
    if wire is not None:
        send = send.astype(wire)
    return keep, send


def swap(array, axis_name, bit):
    return lax.ppermute(array, axis_name, bit_pairs(axis_name, bit))


def bits_of(axis_name):
    return lax.axis_size(axis_name).bit_length() - 1


def scatter_sum(array, axis_name, axis):
    count = bits_of(axis_name)
    shape = array.shape
    length = shape[axis] >> count
    current = array.reshape(shape[:axis] + (2,) * count + (length,) + shape[axis + 1 :])
    for bit in reversed(range(count)):
        keep, send = halve(current, axis_name, bit, axis)
        current = keep + swap(send, axis_name, bit)
    return current


def gather(array, axis_name, axis):
    for bit in range(bits_of(axis_name)):
        mine = (lax.axis_index(axis_name) >> bit) & 1
        got = swap(array, axis_name, bit)
        array = jnp.where(
            mine == 0,
            jnp.concatenate([array, got], axis=axis),
            jnp.concatenate([got, array], axis=axis),
        )
    return array


def after(array, arrived):
    return lax.optimization_barrier((array, arrived))[0]


def shards(
    tokens,
    gate_up_weight,
    down_weight,
    shrink_store,
    expand_store,
    block_adapter,
    block_live,
    adapter_slot,
):
    steps, total_rows, width_local = tokens.shape
    units = gate_up_weight.shape[2]
    pool_count = lax.axis_size("pool")
    tensor_count = lax.axis_size("tensor")
    me = lax.axis_index("pool")
    core = lax.axis_index("tensor")
    kinds = gate_up_weight.shape[1]
    ranks_local = expand_store.shape[2]
    rank = ranks_local * tensor_count
    units_here = units // tensor_count
    rows_here = total_rows // pool_count
    slots = adapter_slot[block_adapter]

    def columns_of(kind):
        columns = expand_store[0, kind].reshape(ranks_local, pool_count * tensor_count, units_here)
        return columns.transpose(1, 0, 2)

    def exchange_columns(columns):
        got = lax.all_to_all(columns, ("pool", "tensor"), split_axis=0, concat_axis=0, tiled=True)
        return got.reshape(pool_count, rank, units_here)

    outgoing = [columns_of(kind) for kind in range(kinds)]
    pages = [exchange_columns(outgoing[0])]

    first = jnp.einsum(
        "snd,kdc->snkc",
        after(tokens, outgoing[0]),
        shrink_store[0],
        preferred_element_type=jnp.float32,
    )
    mine = jnp.repeat((slots == me).astype(jnp.float32), total_rows // NBLK, axis=1)
    first = first * mine[:, :, None, None]
    first = first.reshape(steps * total_rows, kinds * rank)
    shrunk = scatter_sum(first, "tensor", 0)

    def sum_over(shrunk, some_bits):
        for bit in some_bits:
            shrunk = shrunk + swap(shrunk, "pool", bit)
        return shrunk

    middle = bits_of("pool") // 2
    shrunk = sum_over(shrunk, range(middle))

    weights = after(gate_up_weight, outgoing[0])
    weights = jnp.transpose(weights, (1, 0, 2))
    shrunk, weights, _ = lax.optimization_barrier((shrunk, weights, pages[0]))
    shrunk = sum_over(shrunk, range(middle, bits_of("pool")))
    shrunk = gather(shrunk, "tensor", 0)
    for kind in range(1, kinds):
        outgoing[kind] = after(outgoing[kind], (shrunk, pages[-1]))
        pages.append(exchange_columns(outgoing[kind]))

    flat_tokens = tokens.reshape(steps * total_rows, width_local)
    weights, flat_tokens, _ = lax.optimization_barrier((weights, flat_tokens, outgoing[-1]))
    products = [
        jnp.dot(flat_tokens, weights[kind], preferred_element_type=jnp.float32)
        for kind in range(kinds)
    ]
    products = lax.optimization_barrier(products)
    main = []
    for product in products:
        if tensor_count == 2:
            low_share, high_share = product[:, :units_here], product[:, units_here:]
            got = swap(jnp.where(core == 0, high_share, low_share), "tensor", 0)
            main.append(jnp.where(core == 0, low_share, high_share) + got)
        else:
            main.append(scatter_sum(product, "tensor", 1))

    high = shrunk.astype(jnp.bfloat16)
    low = (shrunk - high.astype(jnp.float32)).astype(jnp.bfloat16)

    bits = bits_of("pool")
    positions = me * rows_here + jnp.arange(rows_here)
    owners = positions // BLK
    half = down_weight.shape[1] // 2
    orders = [list(range(bits)), [1, 0] + list(range(2, bits))]
    parts = []
    for step in range(steps):
        hidden_blocks = []
        for block in range(NBLK):
            page = [
                lax.dynamic_index_in_dim(one, slots[step, block], 0, keepdims=False)
                for one in pages
            ]
            rows = slice(step * total_rows + block * BLK, step * total_rows + (block + 1) * BLK)
            gate, up = [
                main[kind][rows]
                + jnp.dot(
                    jnp.concatenate(
                        [part[rows, kind * rank : (kind + 1) * rank] for part in (high, low)], axis=1
                    ),
                    jnp.concatenate([page[kind], page[kind]], axis=0),
                    preferred_element_type=jnp.float32,
                )
                for kind in range(kinds)
            ]
            hidden_blocks.append((jax.nn.silu(gate) * up).astype(jnp.bfloat16))
        hidden = gather(jnp.concatenate(hidden_blocks, axis=0), "tensor", 1)
        parts.append(
            [
                jnp.dot(
                    hidden,
                    down_weight[:, piece * half : (piece + 1) * half],
                    preferred_element_type=jnp.float32,
                ).reshape((2,) * bits + (rows_here, half))
                for piece in range(2)
            ]
        )

    kept = [[None] * 2 for _ in range(steps)]
    sends = [[None] * 2 for _ in range(steps)]
    arrived = [None] * steps

    def prepare(step, stage):
        if stage == 2:
            parts[step] = [jnp.concatenate(parts[step], axis=-1)]
        kept[step] = [None] * len(parts[step])
        sends[step] = [None] * len(parts[step])
        for piece in range(len(parts[step])):
            left = sorted(orders[piece][stage:], reverse=True)
            bit = orders[piece][stage]
            kept[step][piece], sends[step][piece] = halve(
                parts[step][piece], "pool", bit, left.index(bit), jnp.bfloat16
            )

    def exchange_rows(step, stage):
        arrived[step] = [
            swap(sends[step][piece], "pool", orders[piece][stage])
            for piece in range(len(sends[step]))
        ]
        parts[step] = [
            mine + got.astype(jnp.float32) for mine, got in zip(kept[step], arrived[step])
        ]

    for stage in range(bits):
        for step in range(steps):
            prepare(step, stage)
            if stage == 0 and step:
                sends[step] = after(sends[step], arrived[step - 1])
            if stage == 2 and step == 0:
                sends[step] = after(sends[step], later_sends)
            if stage == 1 and step == steps - 1:
                later_sends = list(sends[step])
            exchange_rows(step, stage)
    results = []
    for step in range(steps):
        live = jnp.sum(
            (owners[:, None] == jnp.arange(NBLK)[None, :]) * block_live[step][None, :], axis=1
        )
        keep = (positions % BLK < live).astype(jnp.float32)
        summed = parts[step][0]
        results.append((summed * keep[:, None]).astype(jnp.bfloat16))
    return jnp.stack(results)


def solution(mesh):
    return jax.shard_map(
        shards,
        mesh=mesh,
        in_specs=(
            P(None, None, "tensor"),
            P("tensor", None, "pool"),
            P("pool", "tensor"),
            P("pool", None, "tensor", None),
            P("pool", None, "tensor", None),
            P(),
            P(),
            P(),
        ),
        out_specs=P(None, "pool", "tensor"),
        check_vma=False,
    )
```

```python
import jax
import jax.numpy as jnp
from jax import lax
from jax.sharding import PartitionSpec as P

BLK = 128
NBLK = 2


def bit_pairs(axis_name, bit):
    return [(i, i ^ (1 << bit)) for i in range(lax.axis_size(axis_name))]


def halve(array, axis_name, bit, axis, wire=None):
    mine = (lax.axis_index(axis_name) >> bit) & 1
    keep = lax.dynamic_index_in_dim(array, mine, axis, keepdims=False)
    send = lax.dynamic_index_in_dim(array, 1 - mine, axis, keepdims=False)
    if wire is not None:
        send = send.astype(wire)
    return keep, send


def swap(array, axis_name, bit):
    return lax.ppermute(array, axis_name, bit_pairs(axis_name, bit))


def bits_of(axis_name):
    return lax.axis_size(axis_name).bit_length() - 1


def scatter_sum(array, axis_name, axis):
    count = bits_of(axis_name)
    shape = array.shape
    length = shape[axis] >> count
    current = array.reshape(shape[:axis] + (2,) * count + (length,) + shape[axis + 1 :])
    for bit in reversed(range(count)):
        keep, send = halve(current, axis_name, bit, axis)
        current = keep + swap(send, axis_name, bit)
    return current


def gather(array, axis_name, axis):
    for bit in range(bits_of(axis_name)):
        mine = (lax.axis_index(axis_name) >> bit) & 1
        got = swap(array, axis_name, bit)
        array = jnp.where(
            mine == 0,
            jnp.concatenate([array, got], axis=axis),
            jnp.concatenate([got, array], axis=axis),
        )
    return array


def after(array, arrived):
    return lax.optimization_barrier((array, arrived))[0]


def shards(
    tokens,
    gate_up_weight,
    down_weight,
    shrink_store,
    expand_store,
    block_adapter,
    block_live,
    adapter_slot,
):
    steps, total_rows, width_local = tokens.shape
    units = gate_up_weight.shape[2]
    pool_count = lax.axis_size("pool")
    tensor_count = lax.axis_size("tensor")
    me = lax.axis_index("pool")
    core = lax.axis_index("tensor")
    kinds = gate_up_weight.shape[1]
    ranks_local = expand_store.shape[2]
    rank = ranks_local * tensor_count
    units_here = units // tensor_count
    rows_here = total_rows // pool_count
    slots = adapter_slot[block_adapter]

    def columns_of(kind):
        columns = expand_store[0, kind].reshape(ranks_local, pool_count * tensor_count, units_here)
        return columns.transpose(1, 0, 2)

    def exchange_columns(columns):
        got = lax.all_to_all(columns, ("pool", "tensor"), split_axis=0, concat_axis=0, tiled=True)
        return got.reshape(pool_count, rank, units_here)

    outgoing = [columns_of(kind) for kind in range(kinds)]
    pages = [exchange_columns(outgoing[0])]

    first = jnp.einsum(
        "snd,kdc->snkc",
        after(tokens, outgoing[0]),
        shrink_store[0],
        preferred_element_type=jnp.float32,
    )
    mine = jnp.repeat((slots == me).astype(jnp.float32), total_rows // NBLK, axis=1)
    first = first * mine[:, :, None, None]
    first = first.reshape(steps * total_rows, kinds * rank)
    shrunk = scatter_sum(first, "tensor", 0)

    def sum_over(shrunk, some_bits):
        for bit in some_bits:
            shrunk = shrunk + swap(shrunk, "pool", bit)
        return shrunk

    middle = bits_of("pool") // 2
    shrunk = sum_over(shrunk, range(middle))

    weights = after(gate_up_weight, outgoing[0])
    weights = jnp.transpose(weights, (1, 0, 2))
    block_slots = [[slots[step, block] for block in range(NBLK)] for step in range(steps)]
    shrunk, weights, block_slots, _ = lax.optimization_barrier(
        (shrunk, weights, block_slots, pages[0])
    )
    shrunk = sum_over(shrunk, range(middle, bits_of("pool")))
    shrunk = gather(shrunk, "tensor", 0)
    for kind in range(1, kinds):
        outgoing[kind] = after(outgoing[kind], (shrunk, pages[-1]))
        pages.append(exchange_columns(outgoing[kind]))

    flat_tokens = tokens.reshape(steps * total_rows, width_local)
    weights, flat_tokens, _ = lax.optimization_barrier((weights, flat_tokens, outgoing[-1]))
    products = [
        jnp.dot(flat_tokens, weights[kind], preferred_element_type=jnp.float32)
        for kind in range(kinds)
    ]
    products = lax.optimization_barrier(products)
    main = []
    for product in products:
        if tensor_count == 2:
            low_share, high_share = product[:, :units_here], product[:, units_here:]
            got = swap(jnp.where(core == 0, high_share, low_share), "tensor", 0)
            step_rows = [slice(s * total_rows, (s + 1) * total_rows) for s in range(steps)]
            main.append(
                [
                    jnp.where(core == 0, low_share[rows], high_share[rows]) + got[rows]
                    for rows in step_rows
                ]
            )
        else:
            whole = scatter_sum(product, "tensor", 1)
            main.append([whole[s * total_rows : (s + 1) * total_rows] for s in range(steps)])

    high = shrunk.astype(jnp.bfloat16)
    low = (shrunk - high.astype(jnp.float32)).astype(jnp.bfloat16)

    bits = bits_of("pool")
    positions = me * rows_here + jnp.arange(rows_here)
    owners = positions // BLK
    half = down_weight.shape[1] // 2
    orders = [list(range(bits)), [1, 0] + list(range(2, bits))]
    parts = []
    for step in range(steps):
        hidden_blocks = []
        for block in range(NBLK):
            page = [
                lax.dynamic_index_in_dim(one, block_slots[step][block], 0, keepdims=False)
                for one in pages
            ]
            rows = slice(step * total_rows + block * BLK, step * total_rows + (block + 1) * BLK)
            gate, up = [
                main[kind][step][block * BLK : (block + 1) * BLK]
                + jnp.dot(
                    jnp.concatenate(
                        [part[rows, kind * rank : (kind + 1) * rank] for part in (high, low)], axis=1
                    ),
                    jnp.concatenate([page[kind], page[kind]], axis=0),
                    preferred_element_type=jnp.float32,
                )
                for kind in range(kinds)
            ]
            hidden_blocks.append((jax.nn.silu(gate) * up).astype(jnp.bfloat16))
        hidden = gather(jnp.concatenate(hidden_blocks, axis=0), "tensor", 1)
        parts.append(
            [
                jnp.dot(
                    hidden,
                    down_weight[:, piece * half : (piece + 1) * half],
                    preferred_element_type=jnp.float32,
                ).reshape((2,) * bits + (rows_here, half))
                for piece in range(2)
            ]
        )

    kept = [[None] * 2 for _ in range(steps)]
    sends = [[None] * 2 for _ in range(steps)]
    arrived = [None] * steps

    def prepare(step, stage):
        if stage == 2:
            parts[step] = [jnp.concatenate(parts[step], axis=-1)]
        kept[step] = [None] * len(parts[step])
        sends[step] = [None] * len(parts[step])
        for piece in range(len(parts[step])):
            left = sorted(orders[piece][stage:], reverse=True)
            bit = orders[piece][stage]
            kept[step][piece], sends[step][piece] = halve(
                parts[step][piece], "pool", bit, left.index(bit), jnp.bfloat16
            )

    def exchange_rows(step, stage):
        arrived[step] = [
            swap(sends[step][piece], "pool", orders[piece][stage])
            for piece in range(len(sends[step]))
        ]
        parts[step] = [
            mine + got.astype(jnp.float32) for mine, got in zip(kept[step], arrived[step])
        ]

    for stage in range(bits):
        for step in range(steps):
            prepare(step, stage)
            if stage == 0 and step:
                sends[step] = after(sends[step], arrived[step - 1])
            if stage == 2 and step == 0:
                sends[step] = after(sends[step], later_sends)
            if stage == 1 and step == steps - 1:
                later_sends = list(sends[step])
            exchange_rows(step, stage)
    results = []
    for step in range(steps):
        live = jnp.sum(
            (owners[:, None] == jnp.arange(NBLK)[None, :]) * block_live[step][None, :], axis=1
        )
        keep = (positions % BLK < live).astype(jnp.float32)
        summed = parts[step][0]
        results.append((summed * keep[:, None]).astype(jnp.bfloat16))
    return jnp.stack(results)


def solution(mesh):
    return jax.shard_map(
        shards,
        mesh=mesh,
        in_specs=(
            P(None, None, "tensor"),
            P("tensor", None, "pool"),
            P("pool", "tensor"),
            P("pool", None, "tensor", None),
            P("pool", None, "tensor", None),
            P(),
            P(),
            P(),
        ),
        out_specs=P(None, "pool", "tensor"),
        check_vma=False,
    )
```

```python
import jax
import jax.numpy as jnp
from jax import lax
from jax.sharding import PartitionSpec as P

BLK = 128
NBLK = 2


def bit_pairs(axis_name, bit):
    return [(i, i ^ (1 << bit)) for i in range(lax.axis_size(axis_name))]


def halve(array, axis_name, bit, axis, wire=None):
    mine = ((lax.axis_index(axis_name) >> bit) & 1).astype(jnp.uint32)
    keep = lax.dynamic_index_in_dim(array, mine, axis, keepdims=False)
    send = lax.dynamic_index_in_dim(array, 1 - mine, axis, keepdims=False)
    if wire is not None:
        send = send.astype(wire)
    return keep, send


def swap(array, axis_name, bit):
    return lax.ppermute(array, axis_name, bit_pairs(axis_name, bit))


def bits_of(axis_name):
    return lax.axis_size(axis_name).bit_length() - 1


def scatter_sum(array, axis_name, axis):
    count = bits_of(axis_name)
    shape = array.shape
    length = shape[axis] >> count
    current = array.reshape(shape[:axis] + (2,) * count + (length,) + shape[axis + 1 :])
    for bit in reversed(range(count)):
        keep, send = halve(current, axis_name, bit, axis)
        current = keep + swap(send, axis_name, bit)
    return current


def gather(array, axis_name, axis):
    for bit in range(bits_of(axis_name)):
        mine = (lax.axis_index(axis_name) >> bit) & 1
        got = swap(array, axis_name, bit)
        array = jnp.where(
            mine == 0,
            jnp.concatenate([array, got], axis=axis),
            jnp.concatenate([got, array], axis=axis),
        )
    return array


def after(array, arrived):
    return lax.optimization_barrier((array, arrived))[0]


def shards(
    tokens,
    gate_up_weight,
    down_weight,
    shrink_store,
    expand_store,
    block_adapter,
    block_live,
    adapter_slot,
):
    steps, total_rows, width_local = tokens.shape
    units = gate_up_weight.shape[2]
    pool_count = lax.axis_size("pool")
    tensor_count = lax.axis_size("tensor")
    me = lax.axis_index("pool")
    core = lax.axis_index("tensor")
    kinds = gate_up_weight.shape[1]
    ranks_local = expand_store.shape[2]
    rank = ranks_local * tensor_count
    units_here = units // tensor_count
    rows_here = total_rows // pool_count
    slots = adapter_slot[block_adapter]

    def columns_of(kind):
        columns = expand_store[0, kind].reshape(ranks_local, pool_count * tensor_count, units_here)
        return columns.transpose(1, 0, 2)

    def exchange_columns(columns):
        got = lax.all_to_all(columns, ("pool", "tensor"), split_axis=0, concat_axis=0, tiled=True)
        return got.reshape(pool_count, rank, units_here)

    outgoing = [columns_of(kind) for kind in range(kinds)]
    pages = [exchange_columns(outgoing[0])]

    first = jnp.einsum(
        "snd,kdc->snkc",
        after(tokens, outgoing[0]),
        shrink_store[0],
        preferred_element_type=jnp.float32,
    )
    mine = jnp.repeat((slots == me).astype(jnp.float32), total_rows // NBLK, axis=1)
    first = first * mine[:, :, None, None]
    first = first.reshape(steps * total_rows, kinds * rank)
    shrunk = scatter_sum(first, "tensor", 0)

    def sum_over(shrunk, some_bits):
        for bit in some_bits:
            shrunk = shrunk + swap(shrunk, "pool", bit)
        return shrunk

    middle = bits_of("pool") // 2
    shrunk = sum_over(shrunk, range(middle))

    weights = after(gate_up_weight, outgoing[0])
    weights = jnp.transpose(weights, (1, 0, 2))
    places = slots.astype(jnp.uint32)
    block_slots = [[places[step, block] for block in range(NBLK)] for step in range(steps)]
    shrunk, weights, block_slots, _ = lax.optimization_barrier(
        (shrunk, weights, block_slots, pages[0])
    )
    shrunk = sum_over(shrunk, range(middle, bits_of("pool")))
    shrunk = gather(shrunk, "tensor", 0)
    for kind in range(1, kinds):
        outgoing[kind] = after(outgoing[kind], (shrunk, pages[-1]))
        pages.append(exchange_columns(outgoing[kind]))

    flat_tokens = tokens.reshape(steps * total_rows, width_local)
    weights, flat_tokens, _ = lax.optimization_barrier((weights, flat_tokens, outgoing[-1]))
    products = [
        jnp.dot(flat_tokens, weights[kind], preferred_element_type=jnp.float32)
        for kind in range(kinds)
    ]
    products = lax.optimization_barrier(products)
    main = []
    for product in products:
        if tensor_count == 2:
            low_share, high_share = product[:, :units_here], product[:, units_here:]
            got = swap(jnp.where(core == 0, high_share, low_share), "tensor", 0)
            step_rows = [slice(s * total_rows, (s + 1) * total_rows) for s in range(steps)]
            main.append(
                [
                    jnp.where(core == 0, low_share[rows], high_share[rows]) + got[rows]
                    for rows in step_rows
                ]
            )
        else:
            whole = scatter_sum(product, "tensor", 1)
            main.append([whole[s * total_rows : (s + 1) * total_rows] for s in range(steps)])

    high = shrunk.astype(jnp.bfloat16)
    low = (shrunk - high.astype(jnp.float32)).astype(jnp.bfloat16)

    bits = bits_of("pool")
    positions = me * rows_here + jnp.arange(rows_here)
    owners = positions // BLK
    half = down_weight.shape[1] // 2
    orders = [list(range(bits)), [1, 0] + list(range(2, bits))]
    parts = []
    for step in range(steps):
        hidden_blocks = []
        for block in range(NBLK):
            page = [
                lax.dynamic_index_in_dim(one, block_slots[step][block], 0, keepdims=False)
                for one in pages
            ]
            rows = slice(step * total_rows + block * BLK, step * total_rows + (block + 1) * BLK)
            gate, up = [
                main[kind][step][block * BLK : (block + 1) * BLK]
                + jnp.dot(
                    jnp.concatenate(
                        [part[rows, kind * rank : (kind + 1) * rank] for part in (high, low)], axis=1
                    ),
                    jnp.concatenate([page[kind], page[kind]], axis=0),
                    preferred_element_type=jnp.float32,
                )
                for kind in range(kinds)
            ]
            hidden_blocks.append((jax.nn.silu(gate) * up).astype(jnp.bfloat16))
        hidden = gather(jnp.concatenate(hidden_blocks, axis=0), "tensor", 1)
        parts.append(
            [
                jnp.dot(
                    hidden,
                    down_weight[:, piece * half : (piece + 1) * half],
                    preferred_element_type=jnp.float32,
                ).reshape((2,) * bits + (rows_here, half))
                for piece in range(2)
            ]
        )

    kept = [[None] * 2 for _ in range(steps)]
    sends = [[None] * 2 for _ in range(steps)]
    arrived = [None] * steps

    def prepare(step, stage):
        if stage == 2:
            parts[step] = [jnp.concatenate(parts[step], axis=-1)]
        kept[step] = [None] * len(parts[step])
        sends[step] = [None] * len(parts[step])
        for piece in range(len(parts[step])):
            left = sorted(orders[piece][stage:], reverse=True)
            bit = orders[piece][stage]
            kept[step][piece], sends[step][piece] = halve(
                parts[step][piece], "pool", bit, left.index(bit), jnp.bfloat16
            )

    def exchange_rows(step, stage):
        arrived[step] = [
            swap(sends[step][piece], "pool", orders[piece][stage])
            for piece in range(len(sends[step]))
        ]
        parts[step] = [
            mine + got.astype(jnp.float32) for mine, got in zip(kept[step], arrived[step])
        ]

    for stage in range(bits):
        for step in range(steps):
            prepare(step, stage)
            if stage == 0 and step:
                sends[step] = after(sends[step], arrived[step - 1])
            if stage == 2 and step == 0:
                sends[step] = after(sends[step], later_sends)
            if stage == 1 and step == steps - 1:
                later_sends = list(sends[step])
            exchange_rows(step, stage)
    results = []
    for step in range(steps):
        live = jnp.sum(
            (owners[:, None] == jnp.arange(NBLK)[None, :]) * block_live[step][None, :], axis=1
        )
        keep = (positions % BLK < live).astype(jnp.float32)
        summed = parts[step][0]
        results.append((summed * keep[:, None]).astype(jnp.bfloat16))
    return jnp.stack(results)


def solution(mesh):
    return jax.shard_map(
        shards,
        mesh=mesh,
        in_specs=(
            P(None, None, "tensor"),
            P("tensor", None, "pool"),
            P("pool", "tensor"),
            P("pool", None, "tensor", None),
            P("pool", None, "tensor", None),
            P(),
            P(),
            P(),
        ),
        out_specs=P(None, "pool", "tensor"),
        check_vma=False,
    )
```

```python
import jax
import jax.numpy as jnp
from jax import lax
from jax.sharding import PartitionSpec as P

BLK = 128
NBLK = 2


def bit_pairs(axis_name, bit):
    return [(i, i ^ (1 << bit)) for i in range(lax.axis_size(axis_name))]


def halve(array, axis_name, bit, axis, wire=None):
    mine = ((lax.axis_index(axis_name) >> bit) & 1).astype(jnp.uint32)
    keep = lax.dynamic_index_in_dim(array, mine, axis, keepdims=False)
    send = lax.dynamic_index_in_dim(array, 1 - mine, axis, keepdims=False)
    if wire is not None:
        send = send.astype(wire)
    return keep, send


def swap(array, axis_name, bit):
    return lax.ppermute(array, axis_name, bit_pairs(axis_name, bit))


def bits_of(axis_name):
    return lax.axis_size(axis_name).bit_length() - 1


def scatter_sum(array, axis_name, axis):
    count = bits_of(axis_name)
    shape = array.shape
    length = shape[axis] >> count
    current = array.reshape(shape[:axis] + (2,) * count + (length,) + shape[axis + 1 :])
    for bit in reversed(range(count)):
        keep, send = halve(current, axis_name, bit, axis)
        current = keep + swap(send, axis_name, bit)
    return current


def gather(array, axis_name, axis):
    for bit in range(bits_of(axis_name)):
        mine = (lax.axis_index(axis_name) >> bit) & 1
        got = swap(array, axis_name, bit)
        array = jnp.where(
            mine == 0,
            jnp.concatenate([array, got], axis=axis),
            jnp.concatenate([got, array], axis=axis),
        )
    return array


def after(array, arrived):
    return lax.optimization_barrier((array, arrived))[0]


def shards(
    tokens,
    gate_up_weight,
    down_weight,
    shrink_store,
    expand_store,
    block_adapter,
    block_live,
    adapter_slot,
):
    steps, total_rows, width_local = tokens.shape
    units = gate_up_weight.shape[2]
    pool_count = lax.axis_size("pool")
    tensor_count = lax.axis_size("tensor")
    me = lax.axis_index("pool")
    core = lax.axis_index("tensor")
    kinds = gate_up_weight.shape[1]
    ranks_local = expand_store.shape[2]
    rank = ranks_local * tensor_count
    units_here = units // tensor_count
    rows_here = total_rows // pool_count
    slots = adapter_slot[block_adapter]

    def columns_of(kind):
        columns = expand_store[0, kind].reshape(ranks_local, pool_count * tensor_count, units_here)
        return columns.transpose(1, 0, 2)

    def exchange_columns(columns):
        got = lax.all_to_all(columns, ("pool", "tensor"), split_axis=0, concat_axis=0, tiled=True)
        return got.reshape(pool_count, rank, units_here)

    outgoing = [columns_of(kind) for kind in range(kinds)]
    pages = [exchange_columns(outgoing[0])]

    first = jnp.einsum(
        "snd,kdc->snkc",
        after(tokens, outgoing[0]),
        shrink_store[0],
        preferred_element_type=jnp.float32,
    )
    mine = jnp.repeat((slots == me).astype(jnp.float32), total_rows // NBLK, axis=1)
    first = first * mine[:, :, None, None]
    first = first.reshape(steps * total_rows, kinds * rank)
    shrunk = scatter_sum(first, "tensor", 0)

    def sum_over(shrunk, some_bits):
        for bit in some_bits:
            shrunk = shrunk + swap(shrunk, "pool", bit)
        return shrunk

    middle = bits_of("pool") // 2
    shrunk = sum_over(shrunk, range(middle))

    weights = after(gate_up_weight, outgoing[0])
    weights = jnp.transpose(weights, (1, 0, 2))
    places = slots.astype(jnp.uint32)
    block_slots = [[places[step, block] for block in range(NBLK)] for step in range(steps)]
    shrunk, weights, block_slots, _ = lax.optimization_barrier(
        (shrunk, weights, block_slots, pages[0])
    )
    last = bits_of("pool") - 1
    shrunk = sum_over(shrunk, range(middle, last))
    for kind in range(1, kinds):
        outgoing[kind] = after(outgoing[kind], (shrunk, pages[-1]))
        pages.append(exchange_columns(outgoing[kind]))

    shrunk = gather(sum_over(shrunk, range(last, last + 1)), "tensor", 0)
    flat_tokens = tokens.reshape(steps * total_rows, width_local)
    weights, flat_tokens, _ = lax.optimization_barrier((weights, flat_tokens, outgoing[-1]))
    products = [
        jnp.dot(flat_tokens, weights[kind], preferred_element_type=jnp.float32)
        for kind in range(kinds)
    ]
    products = lax.optimization_barrier(products)
    main = []
    for product in products:
        if tensor_count == 2:
            low_share, high_share = product[:, :units_here], product[:, units_here:]
            got = swap(jnp.where(core == 0, high_share, low_share), "tensor", 0)
            step_rows = [slice(s * total_rows, (s + 1) * total_rows) for s in range(steps)]
            main.append(
                [
                    jnp.where(core == 0, low_share[rows], high_share[rows]) + got[rows]
                    for rows in step_rows
                ]
            )
        else:
            whole = scatter_sum(product, "tensor", 1)
            main.append([whole[s * total_rows : (s + 1) * total_rows] for s in range(steps)])

    high = shrunk.astype(jnp.bfloat16)
    low = (shrunk - high.astype(jnp.float32)).astype(jnp.bfloat16)

    bits = bits_of("pool")
    positions = me * rows_here + jnp.arange(rows_here)
    owners = positions // BLK
    half = down_weight.shape[1] // 2
    orders = [list(range(bits)), [1, 0] + list(range(2, bits))]
    parts = []
    for step in range(steps):
        hidden_blocks = []
        for block in range(NBLK):
            page = [
                lax.dynamic_index_in_dim(one, block_slots[step][block], 0, keepdims=False)
                for one in pages
            ]
            rows = slice(step * total_rows + block * BLK, step * total_rows + (block + 1) * BLK)
            gate, up = [
                main[kind][step][block * BLK : (block + 1) * BLK]
                + jnp.dot(
                    jnp.concatenate(
                        [part[rows, kind * rank : (kind + 1) * rank] for part in (high, low)], axis=1
                    ),
                    jnp.concatenate([page[kind], page[kind]], axis=0),
                    preferred_element_type=jnp.float32,
                )
                for kind in range(kinds)
            ]
            hidden_blocks.append((jax.nn.silu(gate) * up).astype(jnp.bfloat16))
        hidden = gather(jnp.concatenate(hidden_blocks, axis=0), "tensor", 1)
        parts.append(
            [
                jnp.dot(
                    hidden,
                    down_weight[:, piece * half : (piece + 1) * half],
                    preferred_element_type=jnp.float32,
                ).reshape((2,) * bits + (rows_here, half))
                for piece in range(2)
            ]
        )

    kept = [[None] * 2 for _ in range(steps)]
    sends = [[None] * 2 for _ in range(steps)]
    arrived = [None] * steps

    def prepare(step, stage):
        if stage == 2:
            parts[step] = [jnp.concatenate(parts[step], axis=-1)]
        kept[step] = [None] * len(parts[step])
        sends[step] = [None] * len(parts[step])
        for piece in range(len(parts[step])):
            left = sorted(orders[piece][stage:], reverse=True)
            bit = orders[piece][stage]
            kept[step][piece], sends[step][piece] = halve(
                parts[step][piece], "pool", bit, left.index(bit), jnp.bfloat16
            )

    def exchange_rows(step, stage):
        arrived[step] = [
            swap(sends[step][piece], "pool", orders[piece][stage])
            for piece in range(len(sends[step]))
        ]
        parts[step] = [
            mine + got.astype(jnp.float32) for mine, got in zip(kept[step], arrived[step])
        ]

    for stage in range(bits):
        for step in range(steps):
            prepare(step, stage)
            if stage == 0 and step:
                sends[step] = after(sends[step], arrived[step - 1])
            if stage == 2 and step == 0:
                sends[step] = after(sends[step], later_sends)
            if stage == 1 and step == steps - 1:
                later_sends = list(sends[step])
            exchange_rows(step, stage)
    results = []
    for step in range(steps):
        live = jnp.sum(
            (owners[:, None] == jnp.arange(NBLK)[None, :]) * block_live[step][None, :], axis=1
        )
        keep = (positions % BLK < live).astype(jnp.float32)
        summed = parts[step][0]
        results.append((summed * keep[:, None]).astype(jnp.bfloat16))
    return jnp.stack(results)


def solution(mesh):
    return jax.shard_map(
        shards,
        mesh=mesh,
        in_specs=(
            P(None, None, "tensor"),
            P("tensor", None, "pool"),
            P("pool", "tensor"),
            P("pool", None, "tensor", None),
            P("pool", None, "tensor", None),
            P(),
            P(),
            P(),
        ),
        out_specs=P(None, "pool", "tensor"),
        check_vma=False,
    )
```
